32 devices in a mesh: page: 8 (over z, y), stream: 2 (over x), seq: 2 (over core).
Axes of the slice: x: 2, y: 2, z: 4, core: 2. Of those that a mesh axis runs over, the one named last changes fastest.
Arguments:
- tokens: bfloat16 [8, 2, 512, 768], P('page', 'stream', 'seq'), may hold values from -6 to 6
- boxes: int32 [2, 8, 2, 512], P(None, 'page', 'stream', 'seq'), may hold values from 0 to 255
- text_lengths: int32 [8], P('page'), may hold values from 128 to 512, as said below
- language: int32 [8], P('page'), may hold values from 0 to 6
- lang_table: bfloat16 [768, 7], replicated, may hold values from -3 to 3
- w_query: bfloat16 [768, 768], replicated, may hold values from -0.21875 to 0.21875
- b_query: bfloat16 [768], replicated, may hold values from -3 to 3
- w_key: bfloat16 [768, 768], replicated, may hold values from -0.21875 to 0.21875
- w_value: bfloat16 [768, 768], replicated, may hold values from -0.21875 to 0.21875
- b_value: bfloat16 [768], replicated, may hold values from -1.1953125 to 1.1953125
- w_out: bfloat16 [768, 768], replicated, may hold values from -0.625 to 0.625
- b_out: bfloat16 [768], replicated, may hold values from -3 to 3
- norm1_gain: bfloat16 [768], replicated, may hold values from 0.099609375 to 1.8984375
- norm1_bias: bfloat16 [768], replicated, may hold values from -3 to 3
- w_up: bfloat16 [768, 3072], replicated, may hold values from -0.21875 to 0.21875
- b_up: bfloat16 [3072], replicated, may hold values from -3 to 3
- w_down: bfloat16 [3072, 768], replicated, may hold values from -0.21875 to 0.21875
- b_down: bfloat16 [768], replicated, may hold values from -3 to 3
- norm2_gain: bfloat16 [768], replicated, may hold values from 0.099609375 to 1.8984375
- norm2_bias: bfloat16 [768], replicated, may hold values from -3 to 3
- table_pos: bfloat16 [32, 12], replicated, may hold values from -3 to 3
- table_x: bfloat16 [32, 12], replicated, may hold values from -3 to 3
- table_y: bfloat16 [32, 12], replicated, may hold values from -3 to 3
- cotangent: bfloat16 [8, 2, 512, 768], P('page', 'stream', 'seq'), may hold values from -6 to 6
Outputs:
- layer_out: bfloat16 [8, 2, 512, 768], P('page', 'stream', 'seq')
- input_grad: bfloat16 [8, 2, 512, 768], P('page', 'stream', 'seq')
- lang_table_grad: float32 [768, 7], P(('stream', 'seq'))
- w_query_grad: float32 [768, 768], P(('stream', 'seq'))
- b_query_grad: float32 [768], P(('stream', 'seq'))
- w_key_grad: float32 [768, 768], P(('stream', 'seq'))
- w_value_grad: float32 [768, 768], P(('stream', 'seq'))
- b_value_grad: float32 [768], P(('stream', 'seq'))
- w_out_grad: float32 [768, 768], P(('stream', 'seq'))
- b_out_grad: float32 [768], P(('stream', 'seq'))
- norm1_gain_grad: float32 [768], P(('stream', 'seq'))
- norm1_bias_grad: float32 [768], P(('stream', 'seq'))
- w_up_grad: float32 [768, 3072], P(('stream', 'seq'))
- b_up_grad: float32 [3072], P(('stream', 'seq'))
- w_down_grad: float32 [3072, 768], P(('stream', 'seq'))
- b_down_grad: float32 [768], P(('stream', 'seq'))
- norm2_gain_grad: float32 [768], P(('stream', 'seq'))
- norm2_bias_grad: float32 [768], P(('stream', 'seq'))
- table_pos_grad: float32 [32, 12], P(('stream', 'seq'))
- table_x_grad: float32 [32, 12], P(('stream', 'seq'))
- table_y_grad: float32 [32, 12], P(('stream', 'seq'))
The draws below stay inside these ranges and needn't reach their ends.
Inputs may be any that keep to these rules, and one draw needn't show every extreme that they name: `text_lengths`: at least one page in every draw has all 512 text slots live.
All inputs are finite; a program needn't handle non-finite values.
Results may differ from the reference program's by a relative error of at most 0.023.
Values may be sent and summed in bfloat16 or wider, within the bound.
No kernel may reach another device: no remote copies, remote signals or barrier semaphores. Data moves between devices by JAX's collectives and lax.ppermute only.
A program may use at most 128 MiB of HBM per device.

```python
import jax
import jax.numpy as jnp
from jax import lax

D = 768
HEADS = 12
HEAD_DIM = 64
FF = 3072
NB = 32
LANGS = 7
TOK_DEV = 256
PAGES = 8
TEXT_LEN = 512
PAGE_LEN = 1024
N_STREAM = 2


def draw_text_lengths(key, part):
    key = jax.random.fold_in(key, 11)
    draw_key, pick_key = jax.random.split(key)
    drawn = jax.random.randint(draw_key, (PAGES,), TOK_DEV // 2, TEXT_LEN + 1)
    chosen = jax.random.randint(pick_key, (), 0, PAGES)
    return jnp.where(jnp.arange(PAGES) == chosen, TEXT_LEN, drawn).astype(jnp.int32)


def with_ends(values, rng, low, top_value):
    longest = values.shape.index(max(values.shape))
    spots = []
    for shift in (0, 1):
        where = [jax.random.randint(jax.random.fold_in(rng, axis), (), 0, length) for axis, length in enumerate(values.shape)]
        where[longest] = (where[longest] + shift) % values.shape[longest]
        spots.append(tuple(where))
    return values.at[spots[0]].set(low).at[spots[1]].set(top_value)


def levels(stream_key, dims, cuts, least, largest):
    level, own = 1.0, jax.random.fold_in(stream_key, 6)
    for dim, parts in cuts:
        steps = jnp.exp(jax.random.uniform(jax.random.fold_in(own, dim), (parts,), jnp.float32, least / len(cuts), largest / len(cuts)))
        level = level * jnp.repeat(steps, dims[dim] // parts).reshape([-1 if axis == dim else 1 for axis in range(len(dims))])
    return level


def gaussian(stream_key, extent, deviation, bound, cuts=(), kind=jnp.bfloat16):
    values = deviation * jax.random.normal(stream_key, extent, jnp.float32)
    if cuts:
        values = values * levels(stream_key, extent, cuts, -0.22, 0.18)
    return jnp.clip(values, -bound, bound).astype(kind)


def setup_inputs(seed: int = 0) -> dict:
    keys = jax.random.split(jax.random.key(seed), 25)
    return {
        "tokens": gaussian(keys[0], (PAGES, N_STREAM, TEXT_LEN, D), 1.0, 6.0, ((0, 8), (1, 2), (2, 2))),
        "boxes": with_ends(jax.random.randint(keys[1], (2, PAGES, N_STREAM, TEXT_LEN), 0, 8 * NB), jax.random.fold_in(keys[1], 1), 0, (8 * NB) - 1).astype(jnp.int32),
        "text_lengths": draw_text_lengths(jax.random.fold_in(keys[24], 71), 0),
        "language": with_ends(jax.random.randint(keys[3], (PAGES,), 0, LANGS), jax.random.fold_in(keys[3], 1), 0, LANGS - 1).astype(jnp.int32),
        "lang_table": gaussian(keys[4], (D, LANGS), 0.5, 3.0),
        "w_query": gaussian(keys[5], (D, D), D ** -0.5, 0.21875),
        "b_query": gaussian(keys[6], (D,), 0.5, 3.0),
        "w_key": gaussian(keys[7], (D, D), D ** -0.5, 0.21875),
        "w_value": gaussian(keys[8], (D, D), D ** -0.5, 0.21875),
        "b_value": gaussian(keys[9], (D,), 0.2, 1.1953125),
        "w_out": gaussian(keys[10], (D, D), (D // 8) ** -0.5, 0.625),
        "b_out": gaussian(keys[11], (D,), 0.5, 3.0),
        "norm1_gain": jnp.clip(1.0 + 0.18 * jax.random.normal(keys[12], (D,), jnp.float32), 0.099609375, 1.8984375).astype(jnp.bfloat16),
        "norm1_bias": gaussian(keys[13], (D,), 0.5, 3.0),
        "w_up": gaussian(keys[14], (D, FF), D ** -0.5, 0.21875),
        "b_up": gaussian(keys[15], (FF,), 0.5, 3.0),
        "w_down": gaussian(keys[16], (FF, D), (FF // 4) ** -0.5, 0.21875),
        "b_down": gaussian(keys[17], (D,), 0.5, 3.0),
        "norm2_gain": jnp.clip(1.0 + 0.18 * jax.random.normal(keys[18], (D,), jnp.float32), 0.099609375, 1.8984375).astype(jnp.bfloat16),
        "norm2_bias": gaussian(keys[19], (D,), 0.5, 3.0),
        "table_pos": gaussian(keys[20], (NB, HEADS), 0.5, 3.0),
        "table_x": gaussian(keys[21], (NB, HEADS), 0.5, 3.0),
        "table_y": gaussian(keys[22], (NB, HEADS), 0.5, 3.0),
        "cotangent": gaussian(keys[23], (PAGES, N_STREAM, TEXT_LEN, D), 1.0, 6.0, ((0, 8), (1, 2), (2, 2))),
    }


norm_eps = 1e-05
masked_score = -1000000000.0
level_step = 8
highest = lax.Precision.HIGHEST

@jax.custom_vjp
def low(v):
    return lax.optimization_barrier(v.astype(jnp.bfloat16)).astype(jnp.float32)

@jax.custom_vjp
def low_back(v):
    return v

def low_keep(v):
    return (low(v), None)

def low_pass(kept, grad):
    return (grad,)

def back_keep(v):
    return (v, None)

def back_low(kept, grad):
    return (low(grad),)
low.defvjp(low_keep, low_pass)
low_back.defvjp(back_keep, back_low)

def layer_norm(resid, gain, shift):
    center = resid - lax.optimization_barrier(jnp.mean(resid, axis=-1, keepdims=True))
    spread = lax.optimization_barrier(jnp.mean(center * center, axis=-1, keepdims=True))
    return center * lax.rsqrt(spread + norm_eps) * gain + shift

def bucket_of(query_levels, key_levels, buckets):
    half_span = buckets // 2
    return jnp.clip(key_levels[None, :] - query_levels[:, None], -half_span, half_span - 1) + half_span

def split_heads(matrix):
    return matrix.reshape(PAGE_LEN, HEADS, HEAD_DIM).transpose(1, 0, 2)

def page_forward(weights, page_x, page_boxes, text_count, lang_id):
    lang_table, w_query, b_query, w_key, w_value, b_value, w_out, b_out, norm1_gain, norm1_bias, w_up, b_up, w_down, b_down, norm2_gain, norm2_bias, table_pos, table_x, table_y = weights
    start_in = page_x + lang_table[:, lang_id][None, :]
    start_low = low(start_in)
    query = low(low_back(jnp.dot(start_low, w_query, precision=highest) + b_query))
    keys_all = low(low_back(jnp.dot(start_low, w_key, precision=highest)))
    values_all = low(low_back(jnp.dot(start_low, w_value, precision=highest) + b_value))
    place = jnp.arange(PAGE_LEN, dtype=jnp.int32)
    pos_index = bucket_of(place // level_step, place // level_step, NB)
    x_levels = page_boxes[0] // level_step
    y_levels = page_boxes[1] // level_step
    x_index = bucket_of(x_levels, x_levels, NB)
    y_index = bucket_of(y_levels, y_levels, NB)
    key_valid = jnp.logical_or(place >= TEXT_LEN, place < text_count)
    score_scale = HEAD_DIM ** (-0.5)

    def head_attend(head_items):
        query_head, key_head, value_head, pos_row, x_row, y_row = head_items
        scores = jnp.dot(query_head, key_head.T, precision=highest) * score_scale
        scores = scores + (pos_row[pos_index] + x_row[x_index] + y_row[y_index])
        scores = low_back(jnp.where(key_valid[None, :], scores, masked_score))
        attn_weights = jax.nn.softmax(scores, axis=-1)
        return jnp.dot(low(attn_weights), value_head, precision=highest)
    context = lax.map(jax.checkpoint(head_attend), (split_heads(query), split_heads(keys_all), split_heads(values_all), table_pos.T, table_x.T, table_y.T))
    context = low(low_back(context.transpose(1, 0, 2).reshape(PAGE_LEN, D)))
    attn_out = low_back(jnp.dot(context, w_out, precision=highest) + b_out)
    hidden_one = layer_norm(start_in + attn_out, norm1_gain, norm1_bias)
    up_value = low_back(jnp.dot(low(hidden_one), w_up, precision=highest) + b_up)
    gelu_low = low(jax.nn.gelu(up_value, approximate=False))
    down_value = low_back(jnp.dot(gelu_low, w_down, precision=highest) + b_down)
    return layer_norm(hidden_one + down_value, norm2_gain, norm2_bias)

def reference(tokens, boxes, text_lengths, language, lang_table, w_query, b_query, w_key, w_value, b_value, w_out, b_out, norm1_gain, norm1_bias, w_up, b_up, w_down, b_down, norm2_gain, norm2_bias, table_pos, table_x, table_y, cotangent):
    weights = tuple((weight_in.astype(jnp.float32) for weight_in in (lang_table, w_query, b_query, w_key, w_value, b_value, w_out, b_out, norm1_gain, norm1_bias, w_up, b_up, w_down, b_down, norm2_gain, norm2_bias, table_pos, table_x, table_y)))
    page_tokens = tokens.astype(jnp.float32).reshape(PAGES, PAGE_LEN, D)
    page_cots = cotangent.astype(jnp.float32).reshape(PAGES, PAGE_LEN, D)
    page_boxes = jnp.transpose(boxes, (1, 0, 2, 3)).reshape(PAGES, 2, PAGE_LEN)

    def page_step(totals, page_items):
        tokens_in, boxes_in, text_count, lang_id, cot_in = page_items

        def page_run(weights_in, tokens_here):
            return page_forward(weights_in, tokens_here, boxes_in, text_count, lang_id)
        out_page, page_back = jax.vjp(page_run, weights, tokens_in)
        grad_weights, grad_tokens = page_back(cot_in)
        totals = jax.tree.map(lambda running, addend: running + addend, totals, grad_weights)
        return (totals, (out_page.astype(jnp.bfloat16), grad_tokens.astype(jnp.bfloat16)))
    zero_grads = jax.tree.map(jnp.zeros_like, weights)
    totals, (outs_all, grads_all) = lax.scan(page_step, zero_grads, (page_tokens, page_boxes, text_lengths, language, page_cots))
    layer_out = outs_all.reshape(PAGES, N_STREAM, TEXT_LEN, D)
    input_grad = grads_all.reshape(PAGES, N_STREAM, TEXT_LEN, D)
    return (layer_out, input_grad, totals[0], totals[1], totals[2], totals[3], totals[4], totals[5], totals[6], totals[7], totals[8], totals[9], totals[10], totals[11], totals[12], totals[13], totals[14], totals[15], totals[16], totals[17], totals[18])
```

```python
import jax
import jax.numpy as jnp
import numpy as np
from jax import lax
from jax.experimental import pallas as pl
from jax.experimental.pallas import tpu as pltpu
from jax.sharding import PartitionSpec as P

HEADS = 12
norm_eps = 1e-05
masked_score = -1000000000.0
level_step = 8
f32 = jnp.float32
bf16 = jnp.bfloat16
MB = 1 << 20
PAGE_AXES = ("page", "stream", "seq")


def dot_nn(left, right):
    return lax.dot_general(left, right, (((1,), (0,)), ((), ())), preferred_element_type=f32)


def dot_nt(left, right):
    return lax.dot_general(left, right, (((1,), (1,)), ((), ())), preferred_element_type=f32)


def dot_tn(left, right):
    return lax.dot_general(left, right, (((0,), (0,)), ((), ())), preferred_element_type=f32)


def params(vmem_mb, steps=1):
    return pltpu.CompilerParams(
        vmem_limit_bytes=vmem_mb * MB, dimension_semantics=("arbitrary",) * steps
    )


def lane_low(rows=1):
    return lax.broadcasted_iota(jnp.int32, (rows, 128), 1) < 64


def bias_kernel(tab_ref, out_ref):
    head = pl.program_id(0)

    def fill(rows, lanes, first):
        row = lax.broadcasted_iota(jnp.int32, (rows, lanes), 0)
        lane = lax.broadcasted_iota(jnp.int32, (rows, lanes), 1)
        if rows == 32:
            lane = lane % 32
        index = jnp.clip(lane - row, -16, 15) + 16
        total = jnp.zeros((rows, lanes), f32)
        for bucket in range(32):
            total = jnp.where(index == bucket, tab_ref[first + bucket, head], total)
        return total

    part = (lax.broadcasted_iota(jnp.int32, (32, 128), 1) // 32) % 2
    out_ref[0, 0:32, 0:128] = jnp.where(part == 0, fill(32, 128, 0), 0.0).astype(bf16)
    out_ref[0, 32:64, 0:128] = jnp.where(part == 1, fill(32, 128, 32), 0.0).astype(bf16)
    out_ref[0, 64:128, 0:128] = jnp.zeros((64, 128), bf16)
    out_ref[0, 0:128, 128:256] = jnp.zeros((128, 128), bf16)
    out_ref[0, 128:256, 0:128] = jnp.zeros((128, 128), bf16)
    out_ref[0, 128:256, 128:256] = fill(128, 128, 64).astype(bf16)


def bias_mats(tables):
    return pl.pallas_call(
        bias_kernel,
        grid=(HEADS,),
        in_specs=[pl.BlockSpec(memory_space=pltpu.SMEM)],
        out_specs=pl.BlockSpec((1, 256, 256), lambda i: (i, 0, 0)),
        out_shape=jax.ShapeDtypeStruct((HEADS, 256, 256), bf16),
        compiler_params=params(16),
    )(tables)


def norm_parts(resid):
    center = resid - jnp.mean(resid, axis=-1, keepdims=True)
    spread = jnp.mean(center * center, axis=-1, keepdims=True)
    rstd = lax.rsqrt(spread + norm_eps)
    return center * rstd, rstd


def attn_fwd_kernel(
    q_ref, k_ref, v_ref, hot_ref, b_ref, mask_ref, h0_ref, wout_ref, vec_ref,
    ctx_ref, r1_ref, h1_ref, h1r_ref, ctx_s,
):
    step = pl.program_id(0)
    rows = q_ref.shape[0]
    low = lane_low()
    q_pair = q_ref[...] * bf16(0.125)
    k_pair = k_ref[...]
    v_pair = v_ref[...]
    hot_xy = hot_ref[:, 0:128]
    hot_pos = hot_ref[:, 128:256]
    hot_own = hot_ref[0:rows, :]
    one = jnp.ones((), bf16)
    outs = []
    for e in range(2):
        mine = low if e == 0 else jnp.logical_not(low)
        side = dot_nn(hot_own, b_ref[e]).astype(bf16)
        q_aug = jnp.concatenate([jnp.where(mine, q_pair, side[:, 0:128]), side[:, 128:256]], axis=1)
        k_aug = jnp.concatenate([jnp.where(mine, k_pair, hot_xy), hot_pos], axis=1)
        score = dot_nt(q_aug, k_aug) + mask_ref[...]
        top = jnp.max(score, axis=1, keepdims=True)
        weight = jnp.exp(score - top).astype(bf16)
        acc = dot_nn(weight, jnp.where(mine, v_pair, one))
        outs.append(acc / pltpu.roll(acc, 64, 1))
    ctx = jnp.where(low, outs[0], outs[1]).astype(bf16)
    ctx_ref[...] = ctx
    ctx_s[step] = ctx

    @pl.when(step == pl.num_programs(0) - 1)
    def _():
        acc = jnp.zeros(r1_ref.shape, f32)
        for i in range(HEADS // 2):
            acc = acc + dot_nn(ctx_s[i], wout_ref[128 * i : 128 * (i + 1), :])
        resid = h0_ref[...] + (acc + vec_ref[0:1, :])
        r1_ref[...] = resid
        hidden = norm_parts(resid)[0] * vec_ref[1:2, :] + vec_ref[2:3, :]
        h1_ref[...] = hidden
        h1r_ref[...] = hidden.astype(bf16)


def attn_fwd(q, k, v, hot, bias, mask, h0, w_out, vec):
    rows, width = q.shape
    keys = k.shape[0]
    full = lambda shape: pl.BlockSpec(shape, lambda i: (0,) * len(shape))
    return pl.pallas_call(
        attn_fwd_kernel,
        grid=(HEADS // 2,),
        in_specs=[
            pl.BlockSpec((rows, 128), lambda i: (0, i)),
            pl.BlockSpec((keys, 128), lambda i: (0, i)),
            pl.BlockSpec((keys, 128), lambda i: (0, i)),
            full((keys, 256)),
            pl.BlockSpec((2, 256, 256), lambda i: (i, 0, 0)),
            full((1, keys)),
            full((rows, width)),
            full((width, width)),
            full((8, width)),
        ],
        out_specs=[
            pl.BlockSpec((rows, 128), lambda i: (0, i)),
            full((rows, width)),
            full((rows, width)),
            full((rows, width)),
        ],
        out_shape=[
            jax.ShapeDtypeStruct((rows, width), bf16),
            jax.ShapeDtypeStruct((rows, width), f32),
            jax.ShapeDtypeStruct((rows, width), f32),
            jax.ShapeDtypeStruct((rows, width), bf16),
        ],
        scratch_shapes=[pltpu.VMEM((HEADS // 2, rows, 128), bf16)],
        compiler_params=params(48),
    )(q, k, v, hot, bias, mask, h0, w_out, vec)


def gelu_parts(u):
    phi = 0.5 + 0.5 * lax.erf(u * 0.7071067811865476)
    dens = jnp.exp(-0.5 * (u * u)) * 0.3989422804014327
    return u * phi, phi + u * dens


def norm_back(grad, xhat, rstd, gain):
    scaled = grad * gain
    mean_a = jnp.mean(scaled, axis=-1, keepdims=True)
    mean_b = jnp.mean(scaled * xhat, axis=-1, keepdims=True)
    return rstd * (scaled - mean_a - xhat * mean_b)


def col_sum(values):
    return jnp.sum(values, axis=0, keepdims=True)


def ffn_fwd_kernel(
    h1r_ref, wup_ref, bup_ref, wdown_ref, h1_ref, cot_ref, vec_ref,
    out_ref, dy_ref, dr2_ref, gp_ref, sums_ref, acc_s,
):
    step = pl.program_id(0)
    u = dot_nn(h1r_ref[...], wup_ref[...]) + bup_ref[...]
    g, slope = gelu_parts(u)
    gp_ref[...] = slope.astype(bf16)
    part = dot_nn(g.astype(bf16), wdown_ref[...])

    @pl.when(step == 0)
    def _():
        acc_s[...] = part

    @pl.when(step > 0)
    def _():
        acc_s[...] += part

    @pl.when(step == pl.num_programs(0) - 1)
    def _():
        resid = h1_ref[...] + (acc_s[...] + vec_ref[0:1, :])
        gain = vec_ref[1:2, :]
        xhat, rstd = norm_parts(resid)
        out_ref[...] = (xhat * gain + vec_ref[2:3, :]).astype(bf16)
        grad = cot_ref[...].astype(f32)
        dr2 = norm_back(grad, xhat, rstd, gain)
        dr2_ref[...] = dr2
        dy = dr2.astype(bf16)
        dy_ref[...] = dy
        sums_ref[0:1, :] = col_sum(dy.astype(f32))
        sums_ref[1:2, :] = col_sum(grad * xhat)
        sums_ref[2:3, :] = col_sum(grad)
        sums_ref[3:8, :] = jnp.zeros((5, sums_ref.shape[1]), f32)


def ffn_fwd(h1r, w_up, b_up, w_down, h1, cot, vec):
    rows, width = h1.shape
    hidden = w_up.shape[1]
    part = width
    full = lambda shape: pl.BlockSpec(shape, lambda i: (0,) * len(shape))
    return pl.pallas_call(
        ffn_fwd_kernel,
        grid=(hidden // part,),
        in_specs=[
            full((rows, width)),
            pl.BlockSpec((width, part), lambda i: (0, i)),
            pl.BlockSpec((1, part), lambda i: (0, i)),
            pl.BlockSpec((part, width), lambda i: (i, 0)),
            full((rows, width)),
            full((rows, width)),
            full((8, width)),
        ],
        out_specs=[
            full((rows, width)),
            full((rows, width)),
            full((rows, width)),
            pl.BlockSpec((rows, part), lambda i: (0, i)),
            full((8, width)),
        ],
        out_shape=[
            jax.ShapeDtypeStruct((rows, width), bf16),
            jax.ShapeDtypeStruct((rows, width), bf16),
            jax.ShapeDtypeStruct((rows, width), f32),
            jax.ShapeDtypeStruct((rows, hidden), bf16),
            jax.ShapeDtypeStruct((8, width), f32),
        ],
        scratch_shapes=[pltpu.VMEM((rows, width), f32)],
        compiler_params=params(48),
    )(h1r, w_up, b_up, w_down, h1, cot, vec)


def ffn_bwd_kernel(
    dy_ref, wdown_ref, gp_ref, wup_ref, dr2_ref, r1_ref, vec_ref,
    dr1_ref, da_ref, sums_ref, acc_s,
):
    step = pl.program_id(0)
    du = (dot_nt(dy_ref[...], wdown_ref[...]) * gp_ref[...].astype(f32)).astype(bf16)
    part = dot_nt(du, wup_ref[...])

    @pl.when(step == 0)
    def _():
        acc_s[...] = part

    @pl.when(step > 0)
    def _():
        acc_s[...] += part

    @pl.when(step == pl.num_programs(0) - 1)
    def _():
        grad = dr2_ref[...] + acc_s[...]
        xhat, rstd = norm_parts(r1_ref[...])
        dr1 = norm_back(grad, xhat, rstd, vec_ref[1:2, :])
        dr1_ref[...] = dr1
        da = dr1.astype(bf16)
        da_ref[...] = da
        sums_ref[0:1, :] = col_sum(da.astype(f32))
        sums_ref[1:2, :] = col_sum(grad * xhat)
        sums_ref[2:3, :] = col_sum(grad)
        sums_ref[3:4, :] = col_sum(dr1)
        sums_ref[4:8, :] = jnp.zeros((4, sums_ref.shape[1]), f32)


def ffn_bwd(dy, w_down, gp, w_up, dr2, r1, vec):
    rows, width = dr2.shape
    hidden = w_up.shape[1]
    part = width
    full = lambda shape: pl.BlockSpec(shape, lambda i: (0,) * len(shape))
    return pl.pallas_call(
        ffn_bwd_kernel,
        grid=(hidden // part,),
        in_specs=[
            full((rows, width)),
            pl.BlockSpec((part, width), lambda i: (i, 0)),
            pl.BlockSpec((rows, part), lambda i: (0, i)),
            pl.BlockSpec((width, part), lambda i: (0, i)),
            full((rows, width)),
            full((rows, width)),
            full((8, width)),
        ],
        out_specs=[full((rows, width)), full((rows, width)), full((8, width))],
        out_shape=[
            jax.ShapeDtypeStruct((rows, width), f32),
            jax.ShapeDtypeStruct((rows, width), bf16),
            jax.ShapeDtypeStruct((8, width), f32),
        ],
        scratch_shapes=[pltpu.VMEM((rows, width), f32)],
        compiler_params=params(48),
    )(dy, w_down, gp, w_up, dr2, r1, vec)


def ffn_again_kernel(d_ref, h1_ref, wup_ref, bup_ref, g_ref, gp_ref):
    u = dot_nn(h1_ref[...], wup_ref[...]) + bup_ref[...]
    g, slope = gelu_parts(u)
    g_ref[...] = g.astype(bf16)
    gp_ref[...] = slope.astype(bf16)


def ffn_again(quarter, h1_all, w_up, b_up):
    keys, width = h1_all.shape
    part = w_up.shape[1] // 4
    rows = keys // 4
    return pl.pallas_call(
        ffn_again_kernel,
        grid_spec=pltpu.PrefetchScalarGridSpec(
            num_scalar_prefetch=1,
            grid=(4,),
            in_specs=[
                pl.BlockSpec((rows, width), lambda i, d: (i, 0)),
                pl.BlockSpec((width, part), lambda i, d: (0, d[0])),
                pl.BlockSpec((1, part), lambda i, d: (0, d[0])),
            ],
            out_specs=[
                pl.BlockSpec((rows, part), lambda i, d: (i, 0)),
                pl.BlockSpec((rows, part), lambda i, d: (i, 0)),
            ],
        ),
        out_shape=[jax.ShapeDtypeStruct((keys, part), bf16)] * 2,
        compiler_params=params(48),
    )(quarter, h1_all, w_up, b_up)


def attn_bwd_kernel(d_ref, p_ref, dc_ref, hot_ref, b_ref, mask_ref, dp_ref, db_ref):
    low = lane_low()
    zero = jnp.zeros((), bf16)
    kv = p_ref[:, 0:128]
    hot_xy = hot_ref[:, 0:128]
    hot_pos = hot_ref[:, 128:256]
    k_aug = jnp.concatenate([jnp.where(low, kv, hot_xy), hot_pos], axis=1)
    k_aug_t = k_aug.T
    v_only = jnp.where(low, zero, kv)
    keys = p_ref.shape[0]
    acc_kv = jnp.zeros((keys, 128), f32)
    acc_b = jnp.zeros((256, 256), f32)
    for block in range(4):
        part = slice(256 * block, 256 * (block + 1))
        q_only = p_ref[part, 128:256] * bf16(0.125)
        hot_q = hot_ref[part, :]
        dc = dc_ref[part, :]
        side = dot_nn(hot_q, b_ref[0]).astype(bf16)
        q_aug = jnp.concatenate(
            [jnp.where(low, q_only, side[:, 0:128]), side[:, 128:256]], axis=1
        )
        score = dot_nt(k_aug, q_aug) + mask_ref[...]
        top = jnp.max(score, axis=0, keepdims=True)
        weight = jnp.exp(score - top)
        weight = weight * (1.0 / jnp.sum(weight, axis=0, keepdims=True))
        dweight = dot_nt(v_only, dc)
        inner = jnp.sum(weight * dweight, axis=0, keepdims=True)
        dscore = (weight * (dweight - inner)).astype(bf16)
        acc_kv = acc_kv + (dot_nn(dscore, q_only) + dot_nn(weight.astype(bf16), dc))
        dq_aug_t = dot_nn(k_aug_t, dscore)
        dq = dq_aug_t[0:128, :].T * 0.125
        dp_ref[part, 128:256] = jnp.where(low, dq, 0.0).astype(bf16)
        acc_b = acc_b + dot_nn(dq_aug_t.astype(bf16), hot_q)
    dp_ref[:, 0:128] = acc_kv.astype(bf16)
    db_ref[0] = acc_b


def attn_bwd(quarter, p_all, dc_all, hot, bias, mask_col):
    keys = p_all.shape[0]
    heads = HEADS // 4
    full = lambda shape: pl.BlockSpec(shape, lambda i, d: (0,) * len(shape))
    return pl.pallas_call(
        attn_bwd_kernel,
        grid_spec=pltpu.PrefetchScalarGridSpec(
            num_scalar_prefetch=1,
            grid=(heads,),
            in_specs=[
                pl.BlockSpec((keys, 256), lambda i, d: (0, i)),
                pl.BlockSpec((keys, 128), lambda i, d: (0, i)),
                full((keys, 256)),
                pl.BlockSpec((1, 256, 256), lambda i, d: (d[0] * heads + i, 0, 0)),
                full((keys, 1)),
            ],
            out_specs=[
                pl.BlockSpec((keys, 256), lambda i, d: (0, i)),
                pl.BlockSpec((1, 256, 256), lambda i, d: (i, 0, 0)),
            ],
        ),
        out_shape=[
            jax.ShapeDtypeStruct((keys, heads * 256), bf16),
            jax.ShapeDtypeStruct((heads, 256, 256), f32),
        ],
        compiler_params=params(56),
    )(quarter, p_all, dc_all, hot, bias, mask_col)


def swap(values, axis):
    return lax.ppermute(values, axis, [(0, 1), (1, 0)])


def page_gather(own):
    near = swap(own, "seq")
    far = swap(own, "stream")
    return [own, near, far, swap(far, "seq")]


def bucket_marks(levels):
    index = np.clip(np.arange(levels)[None, :] - np.arange(levels)[:, None], -16, 15) + 16
    return (index[:, :, None] == np.arange(32)).astype(np.float32)


def on_device(
    tokens, boxes, text_lengths, language, lang_table, w_query, b_query, w_key, w_value, b_value,
    w_out, b_out, norm1_gain, norm1_bias, w_up, b_up, w_down, b_down, norm2_gain, norm2_bias,
    table_pos, table_x, table_y, cotangent,
):
    rows = tokens.shape[2]
    width = tokens.shape[3]
    head_dim = width // HEADS
    own_heads = HEADS // 4
    own_cols = own_heads * head_dim
    keys = 4 * rows
    text_len = 2 * rows
    pages = lax.axis_size("page")
    quarter = lax.axis_index(("stream", "seq")).astype(jnp.int32)
    quarter_arr = quarter.reshape(1)

    lang_count = lang_table.shape[1]
    lang_pick = (jnp.arange(lang_count, dtype=jnp.int32) == language[0]).astype(f32)
    lang_column = jnp.sum(lang_table.astype(f32) * lang_pick[None, :], axis=1)
    h0 = tokens[0, 0].astype(f32) + lang_column[None, :]
    h0r = h0.astype(bf16)
    box_rows = jnp.pad(boxes[:, 0, 0, :].astype(bf16), ((0, 14), (0, width - rows)))
    message = jnp.concatenate([h0r, box_rows], axis=0)
    gathered = page_gather(message)
    h0_all = jnp.concatenate([g[:rows] for g in gathered], axis=0)
    box_all = jnp.concatenate([g[rows : rows + 2, :rows] for g in gathered], axis=1)
    box_all = box_all.astype(jnp.int32) // level_step

    place = jnp.concatenate(
        [(quarter ^ b) * rows + jnp.arange(rows, dtype=jnp.int32) for b in range(4)]
    )
    live = jnp.logical_or(place >= text_len, place < text_lengths[0])
    mask = jnp.where(live, 0.0, masked_score).astype(f32)
    lane = jnp.arange(256, dtype=jnp.int32)[None, :]
    want = jnp.where(
        lane >= 128,
        (place // level_step)[:, None] + 128,
        jnp.where(lane % 64 < 32, box_all[0][:, None], box_all[1][:, None] + 32) + (lane // 64) * 64,
    )
    hot = (want == lane).astype(bf16)

    tables = jnp.concatenate([table_x, table_y, table_pos], axis=0).astype(f32)
    bias = bias_mats(tables)

    cut = lambda m: lax.dynamic_slice_in_dim(m, quarter * own_cols, own_cols, axis=m.ndim - 1)
    cut_k, cut_v, cut_q = cut(w_key), cut(w_value), cut(w_query)
    cut_bv, cut_bq = cut(b_value), cut(b_query)
    pad_w = jnp.zeros((width, head_dim), bf16)
    pad_b = jnp.zeros((head_dim,), bf16)
    w_parts, b_parts = [], []
    for j in range(own_heads):
        c = slice(j * head_dim, (j + 1) * head_dim)
        w_parts += [cut_k[:, c], cut_v[:, c], cut_q[:, c], pad_w]
        b_parts += [pad_b, cut_bv[c], cut_bq[c], pad_b]
    w_arr = jnp.concatenate(w_parts, axis=1)
    b_arr = jnp.concatenate(b_parts).astype(f32)

    q_own = (dot_nn(h0r, w_query) + b_query.astype(f32)).astype(bf16)
    k_all = dot_nn(h0_all, w_key).astype(bf16)
    v_all = (dot_nn(h0_all, w_value) + b_value.astype(f32)).astype(bf16)

    def vec_rows(*vectors):
        stacked = jnp.stack(vectors).astype(f32)
        return jnp.pad(stacked, ((0, 8 - len(vectors)), (0, 0)))

    vec_one = vec_rows(b_out, norm1_gain, norm1_bias)
    vec_two = vec_rows(b_down, norm2_gain, norm2_bias)
    ctx, r1, h1, h1r = attn_fwd(
        q_own, k_all, v_all, hot, bias, mask[None, :], h0, w_out, vec_one
    )
    h1_all = jnp.concatenate(page_gather(h1r), axis=0)
    ctx_cols = [
        lax.dynamic_slice_in_dim(ctx, (quarter ^ b) * own_cols, own_cols, axis=1) for b in range(4)
    ]
    ctx_far = [
        swap(ctx_cols[2], "stream"),
        swap(ctx_cols[3], "stream"),
    ]
    ctx_all = jnp.concatenate(
        [ctx_cols[0], swap(ctx_cols[1], "seq"), ctx_far[0], swap(ctx_far[1], "seq")], axis=0
    )

    b_up_row = b_up.astype(f32)[None, :]
    layer_out, dy, dr2, gp, sums_two = ffn_fwd(
        h1r, w_up, b_up_row, w_down, h1, cotangent[0, 0], vec_two
    )
    dy_all = jnp.concatenate(page_gather(dy), axis=0)
    dr1, da, sums_one = ffn_bwd(dy, w_down, gp, w_up, dr2, r1, vec_one)
    da_all = jnp.concatenate(page_gather(da), axis=0)

    g_q, gp_q = ffn_again(quarter_arr, h1_all, w_up, b_up_row)
    part = w_up.shape[1] // 4
    grad_down = dot_tn(g_q, dy_all).astype(bf16)
    down_q = lax.dynamic_slice_in_dim(w_down, quarter * part, part, axis=0)
    du_q = (dot_nt(dy_all, down_q) * gp_q.astype(f32)).astype(bf16)
    grad_b_up = jnp.sum(du_q.astype(f32), axis=0)
    grad_up = dot_tn(h1_all, du_q).astype(bf16)

    out_rows = lax.dynamic_slice_in_dim(w_out, quarter * own_cols, own_cols, axis=0)
    grad_out = dot_tn(ctx_all, da_all).astype(bf16)
    out_pad = jnp.zeros((head_dim, width), bf16)
    out_arr = jnp.concatenate(
        sum(([out_pad, out_rows[j * head_dim : (j + 1) * head_dim]] for j in range(own_heads)), []),
        axis=0,
    )
    dc_all = dot_nt(da_all, out_arr).astype(bf16)
    p_all = (dot_nn(h0_all, w_arr) + b_arr).astype(bf16)
    dp_all, db = attn_bwd(quarter_arr, p_all, dc_all, hot, bias, mask[:, None])

    grad_arr = dot_tn(h0_all, dp_all).astype(bf16)
    dp_sum = jnp.sum(dp_all.astype(f32), axis=0)
    dh0_part = dot_nt(dp_all, w_arr)
    send_near = jnp.concatenate([dh0_part[rows : 2 * rows], dh0_part[3 * rows :]], axis=0)
    got_near = swap(send_near.astype(bf16), "seq").astype(f32)
    far_sum = (dh0_part[2 * rows : 3 * rows] + got_near[rows:]).astype(bf16)
    got_far = swap(far_sum, "stream").astype(f32)
    dh0 = dr1 + ((dh0_part[:rows] + got_near[:rows]) + got_far)
    input_grad = dh0.astype(bf16)

    dp_heads = dp_sum.reshape(own_heads, 4, head_dim)
    grad_b_value = dp_heads[:, 1].reshape(own_cols)
    grad_b_query = dp_heads[:, 2].reshape(own_cols)
    lang_sum = sums_one[3] + jnp.sum(w_arr.astype(f32) * dp_sum[None, :], axis=1)
    grad_lang = lang_sum[:, None] * lang_pick[None, :]
    marks32 = jnp.asarray(bucket_marks(32))
    marks128 = jnp.asarray(bucket_marks(128))
    exact = dict(precision=lax.Precision.HIGHEST)
    grad_x = jnp.einsum("hba,abn->nh", db[:, 64:96, 0:32], marks32, **exact)
    grad_y = jnp.einsum("hba,abn->nh", db[:, 96:128, 32:64], marks32, **exact)
    grad_pos = jnp.einsum("hba,abn->nh", db[:, 128:256, 128:256], marks128, **exact)
    at_own = (jnp.arange(4) == quarter).astype(f32)
    head_at = (jnp.arange(HEADS)[None, :] == quarter * own_heads + jnp.arange(own_heads)[:, None])
    spread = lambda g: jnp.sum(g[:, :, None] * head_at[None].astype(f32), axis=1).reshape(4, -1)
    by_quarter = lambda v: v.reshape(4, -1)
    placed = lambda v: at_own[:, None] * v[None, :]
    small_parts = [
        by_quarter(grad_lang), placed(grad_b_query), placed(grad_b_value),
        by_quarter(sums_one[0]), by_quarter(sums_one[1]), by_quarter(sums_one[2]),
        placed(grad_b_up),
        by_quarter(sums_two[0]), by_quarter(sums_two[1]), by_quarter(sums_two[2]),
        spread(grad_pos), spread(grad_x), spread(grad_y),
    ]
    sizes = [v.shape[1] for v in small_parts]
    small = jnp.concatenate(small_parts, axis=1)
    small = jnp.pad(small, ((0, 0), (0, 4096 - small.shape[1])))

    def all_rows(mine):
        return lax.all_gather(mine, "page", axis=0, tiled=True)

    def sum_rows(values):
        blocks = values.reshape(pages, values.shape[0] // pages, values.shape[1])
        got = lax.all_to_all(blocks, "page", 0, 0)
        return jnp.sum(got.astype(f32), axis=0).astype(bf16)

    def scatter_all(values):
        got = lax.all_to_all(values, PAGE_AXES, 0, 0)
        return got.reshape((pages, 4) + got.shape[1:]).astype(f32)

    def to_owners(values):
        n = values.shape[0] // (4 * pages)
        split = values.reshape(4, pages, n, values.shape[1]).transpose(1, 0, 2, 3)
        return split.reshape(pages * 4, n, values.shape[1])

    res_down = all_rows(sum_rows(grad_down)).astype(f32)
    up_got = jnp.sum(scatter_all(to_owners(grad_up)), axis=0).astype(bf16)
    n = up_got.shape[1]
    res_up = all_rows(up_got.transpose(1, 0, 2).reshape(n, 4 * part)).astype(f32)
    res_out = all_rows(sum_rows(grad_out)).astype(f32)

    cols = own_heads * 3 * head_dim
    arr = grad_arr.reshape(width, own_heads, 4, head_dim)[:, :, :3].reshape(width, cols)
    arr = to_owners(arr)
    small_send = small.reshape(4, pages, -1).transpose(1, 0, 2).reshape(4 * pages, -1, 64)
    small_send = jnp.pad(small_send.astype(bf16), ((0, 0), (0, n - small_send.shape[1]), (0, 0)))
    tail = scatter_all(jnp.concatenate([arr, small_send], axis=2))
    tail = jnp.sum(tail, axis=0)
    small_sum = jnp.sum(tail[:, :, cols:], axis=0)[: 4096 // pages // 64].reshape(1, -1)
    arr_sum = tail[:, :, :cols].reshape(4, n, own_heads, 3, head_dim)
    arr_sum = arr_sum.transpose(1, 3, 0, 2, 4).reshape(n, 3 * width)
    res_arr = all_rows(arr_sum.astype(bf16)).astype(f32)
    res_key, res_value, res_query = (res_arr[:, i * width : (i + 1) * width] for i in range(3))
    res_small = all_rows(small_sum.astype(bf16)).astype(f32).reshape(-1)
    bounds = np.cumsum([0] + sizes)
    items = [res_small[bounds[i] : bounds[i + 1]] for i in range(len(sizes))]
    (s_lang, s_bq, s_bv, s_bout, s_g1, s_s1, s_bup, s_bdown, s_g2, s_s2, s_pos, s_x, s_y) = items
    tab = lambda v: v.reshape(-1, HEADS)
    return (
        layer_out[None, None], input_grad[None, None], s_lang.reshape(-1, lang_count),
        res_query, s_bq, res_key, res_value, s_bv, res_out, s_bout, s_g1, s_s1,
        res_up, s_bup, res_down, s_bdown, s_g2, s_s2, tab(s_pos), tab(s_x), tab(s_y),
    )


def solution(mesh):
    token_spec = P("page", "stream", "seq", None)
    rep = P()
    in_specs = (
        (token_spec, P(None, "page", "stream", "seq"), P("page"), P("page"))
        + (rep,) * 19
        + (token_spec,)
    )
    mat, vec = P(("stream", "seq"), None), P(("stream", "seq"))
    out_specs = (
        token_spec, token_spec, mat, mat, vec, mat, mat, vec, mat, vec, vec, vec,
        mat, vec, mat, vec, vec, vec, mat, mat, mat,
    )
    return jax.shard_map(
        on_device, mesh=mesh, in_specs=in_specs, out_specs=out_specs, check_vma=False
    )
```

```python
import functools

import jax
import jax.numpy as jnp
import numpy as np
from jax import lax
from jax.experimental import pallas as pl
from jax.experimental.pallas import tpu as pltpu
from jax.sharding import PartitionSpec as P

HEADS = 12
BOX_ROWS = 16
norm_eps = 1e-05
masked_score = -1000000000.0
level_step = 8
f32 = jnp.float32
bf16 = jnp.bfloat16
i32 = jnp.int32
MB = 1 << 20
PAGE_AXES = ("page", "stream", "seq")


def dot_nn(left, right):
    return lax.dot_general(left, right, (((1,), (0,)), ((), ())), preferred_element_type=f32)


def dot_nt(left, right):
    return lax.dot_general(left, right, (((1,), (1,)), ((), ())), preferred_element_type=f32)


def dot_tn(left, right):
    return lax.dot_general(left, right, (((0,), (0,)), ((), ())), preferred_element_type=f32)


def params(vmem_mb):
    return pltpu.CompilerParams(
        vmem_limit_bytes=vmem_mb * MB, dimension_semantics=("arbitrary",)
    )


def struct(shape, kind):
    return jax.ShapeDtypeStruct(shape, kind)


def whole(shape):
    return pl.BlockSpec(shape, lambda *at: (0,) * len(shape))


def fixed(shape, at):
    return pl.BlockSpec(shape, lambda *_: at)


def iota(shape, dim):
    return lax.broadcasted_iota(i32, shape, dim)


def lane_low():
    return iota((1, 128), 1) < 64


SMEM = pl.BlockSpec(memory_space=pltpu.SMEM)
VMEM = pl.BlockSpec(memory_space=pltpu.VMEM)


def cost(micros):
    return pl.CostEstimate(
        flops=int(micros * 1.15e9), bytes_accessed=int(micros * 3.69e6), transcendentals=0
    )


def resident(kernel, micros, vmem_mb, args, outs, scratch=(), scalars=1):
    return pl.pallas_call(
        kernel,
        cost_estimate=cost(micros),
        in_specs=[SMEM] * scalars + [VMEM] * (len(args) - scalars),
        out_specs=[VMEM] * len(outs),
        out_shape=[struct(*out) for out in outs],
        scratch_shapes=[pltpu.VMEM(*entry) for entry in scratch],
        compiler_params=pltpu.CompilerParams(vmem_limit_bytes=vmem_mb * MB),
    )(*args)


def after(values, *others):
    return lax.optimization_barrier((values, others))[0]


def prep_kernel(lang_ref, tok_ref, box_ref, table_ref, h0_ref, msg_ref):
    rows, width = h0_ref.shape
    pick = (iota((8, table_ref.shape[1]), 1) == lang_ref[0]).astype(bf16)
    column = dot_nt(pick, table_ref[...])[0:1, :]
    h0 = tok_ref[0, 0].astype(f32) + column
    h0_ref[...] = h0
    msg_ref[0:rows, :] = h0.astype(bf16)
    row = iota((BOX_ROWS, rows), 0)
    box_x = jnp.broadcast_to(box_ref[0, 0], (BOX_ROWS, rows)).astype(f32)
    box_y = jnp.broadcast_to(box_ref[1, 0], (BOX_ROWS, rows)).astype(f32)
    packed = jnp.where(row == 0, box_x, jnp.where(row == 1, box_y, 0.0)).astype(bf16)
    msg_ref[rows : rows + BOX_ROWS, :] = jnp.zeros((BOX_ROWS, width), bf16)
    msg_ref[rows : rows + BOX_ROWS, 0:rows] = packed


def prep(language, tokens, boxes, lang_table):
    rows, width = tokens.shape[2:]
    return pl.pallas_call(
        prep_kernel,
        cost_estimate=cost(1),
        grid=(1,),
        in_specs=[SMEM, whole(tokens.shape), whole(boxes.shape), whole(lang_table.shape)],
        out_specs=[whole((rows, width)), whole((rows + BOX_ROWS, width))],
        out_shape=[struct((rows, width), f32), struct((rows + BOX_ROWS, width), bf16)],
        compiler_params=params(8),
    )(language, tokens, boxes, lang_table)


def bias_kernel(tx_ref, ty_ref, tp_ref, out_ref):
    bucket = jnp.clip(iota((32, 256), 1) - 128, -16, 15) + 16
    marks = (bucket == iota((32, 256), 0)).astype(bf16)
    diag = [dot_tn(ref[...], marks) for ref in (tx_ref, ty_ref, tp_ref)]
    lane = iota((32, 128), 1)

    def shifted(row, rows):
        return pltpu.roll(jnp.broadcast_to(row, (rows, 256)), 0, 1, stride=1, stride_axis=0)[:, 128:256]

    out_ref[...] = jnp.zeros(out_ref.shape, bf16)
    for head in range(HEADS):
        x = jnp.where(lane < 32, shifted(diag[0][head : head + 1, :], 32), 0.0)
        y = jnp.where(lane < 32, shifted(diag[1][head : head + 1, :], 32), 0.0)
        out_ref[head, 0:32, 0:128] = (x + pltpu.roll(x, 64, 1)).astype(bf16)
        out_ref[head, 32:64, 0:128] = (pltpu.roll(y, 32, 1) + pltpu.roll(y, 96, 1)).astype(bf16)
        out_ref[head, 128:256, 128:256] = shifted(diag[2][head : head + 1, :], 128).astype(bf16)


def bias_mats(table_x, table_y, table_pos):
    return resident(
        bias_kernel, 2, 8, (table_x, table_y, table_pos), [((HEADS, 256, 256), bf16)], scalars=0
    )[0]


def pick_kernel(d_ref, wk_ref, wv_ref, wq_ref, vec_ref, wo_ref, warr_ref, barr_ref, oarr_ref):
    head = d_ref[0] * (HEADS // 4) + pl.program_id(0)
    even = (head % 2) == 0
    low = lane_low()

    def arrange(k, v, q):
        k_low = jnp.where(even, k, pltpu.roll(k, 64, 1))
        v_high = jnp.where(even, pltpu.roll(v, 64, 1), v)
        q_low = jnp.where(even, q, pltpu.roll(q, 64, 1))
        return jnp.concatenate([jnp.where(low, k_low, v_high), jnp.where(low, q_low, 0.0)], axis=1)

    warr_ref[...] = arrange(
        wk_ref[...].astype(f32), wv_ref[...].astype(f32), wq_ref[...].astype(f32)
    ).astype(bf16)
    bv = jnp.broadcast_to(vec_ref[7:8, :], (8, 128))
    bq = jnp.broadcast_to(vec_ref[6:7, :], (8, 128))
    barr_ref[...] = arrange(jnp.zeros_like(bv), bv, bq)
    oarr_ref[0:64, :] = jnp.zeros((64, oarr_ref.shape[1]), bf16)
    oarr_ref[64:128, :] = wo_ref[...]


def pick_weights(scalars, w_key, w_value, w_query, vec, w_out):
    width = w_key.shape[0]
    own = HEADS // 4
    pair = lambda i, d: (0, (d[0] * own + i) // 2)
    return pl.pallas_call(
        pick_kernel,
        cost_estimate=cost(2),
        grid_spec=pltpu.PrefetchScalarGridSpec(
            num_scalar_prefetch=1,
            grid=(own,),
            in_specs=[pl.BlockSpec((width, 128), pair)] * 3
            + [pl.BlockSpec((8, 128), pair)]
            + [pl.BlockSpec((64, width), lambda i, d: (d[0] * own + i, 0))],
            out_specs=[
                pl.BlockSpec((width, 256), lambda i, d: (0, i)),
                pl.BlockSpec((8, 256), lambda i, d: (0, i)),
                pl.BlockSpec((128, width), lambda i, d: (i, 0)),
            ],
        ),
        out_shape=[
            struct((width, own * 256), bf16),
            struct((8, own * 256), f32),
            struct((own * 128, width), bf16),
        ],
        compiler_params=params(6),
    )(scalars, w_key, w_value, w_query, vec, w_out)


def proj_kernel(with_query, first, d_ref, a_ref, b_ref, wk_ref, wv_ref, vec_ref, *refs):
    if with_query:
        wq_ref, k_ref, v_ref, hot_ref, h0_ref, q_ref = refs
    else:
        k_ref, v_ref, hot_ref, h0_ref = refs
    rows = a_ref.shape[0] - BOX_ROWS
    lane = iota((rows, 256), 1)
    for n, ref in enumerate((a_ref, b_ref)):
        h0_ref[n * rows : (n + 1) * rows, :] = ref[0:rows, :]
        boxes = ref[rows : rows + BOX_ROWS, 0:rows].astype(f32).T
        level = jnp.floor(boxes * (1.0 / level_step)).astype(i32)
        start = (d_ref[0] ^ (first + n)) * rows
        place = (start + iota((rows, 256), 0)) // level_step + 128
        flat = jnp.where(lane % 64 < 32, level[:, 0:1], level[:, 1:2] + 32) + (lane // 64) * 64
        want = jnp.where(lane >= 128, place, flat)
        hot_ref[n * rows : (n + 1) * rows, :] = (want == lane).astype(bf16)
    h0 = h0_ref[...]
    width = h0.shape[1]
    for c in range(0, width, 256):
        part = slice(c, c + 256)
        k_ref[:, part] = dot_nn(h0, wk_ref[:, part]).astype(bf16)
        v_ref[:, part] = (dot_nn(h0, wv_ref[:, part]) + vec_ref[7:8, part]).astype(bf16)
        if with_query:
            query = dot_nn(h0[0:rows, :], wq_ref[:, part]) + vec_ref[6:7, part]
            q_ref[:, part] = query.astype(bf16) * bf16(0.125)


def project(scalars, msg_a, msg_b, w_key, w_value, vec, first, w_query=None):
    rows = msg_a.shape[0] - BOX_ROWS
    width = msg_a.shape[1]
    keys = 2 * rows
    args = [scalars, msg_a, msg_b, w_key, w_value, vec]
    outs = [((keys, width), bf16), ((keys, width), bf16), ((keys, 256), bf16), ((keys, width), bf16)]
    if w_query is not None:
        args.append(w_query)
        outs.append(((rows, width), bf16))
    kernel = functools.partial(proj_kernel, w_query is not None, first)
    return resident(kernel, 2, 10, args, outs)


def norm_parts(resid):
    center = resid - jnp.mean(resid, axis=-1, keepdims=True)
    spread = jnp.mean(center * center, axis=-1, keepdims=True)
    rstd = lax.rsqrt(spread + norm_eps)
    return center * rstd, rstd


def place_mask(d_ref, rows, first, shape, dim):
    place = (d_ref[0] ^ first) * rows + iota(shape, dim)
    live = jnp.logical_or(place >= 2 * rows, place < d_ref[1])
    return jnp.where(live, 0.0, masked_score).astype(f32)


def pair_scores(e, q_pair, k_pair, hot_own, hot_ref, bias, mask):
    low = lane_low()
    mine = low if e == 0 else jnp.logical_not(low)
    side = dot_nn(hot_own, bias).astype(bf16)
    q_aug = jnp.concatenate([jnp.where(mine, q_pair, side[:, 0:128]), side[:, 128:256]], axis=1)
    k_aug = jnp.concatenate([jnp.where(mine, k_pair, hot_ref[:, 0:128]), hot_ref[:, 128:256]], axis=1)
    return dot_nt(q_aug, k_aug) + mask, mine


def attn_near_kernel(d_ref, q_ref, k_ref, v_ref, hot_ref, b_ref, acc_ref, top_ref):
    rows = q_ref.shape[0]
    low = lane_low()
    mask = jnp.concatenate([place_mask(d_ref, rows, b, (1, rows), 1) for b in (0, 1)], axis=1)
    hot_own = hot_ref[0:rows, :]
    for i in range(HEADS // 2):
        pair = slice(128 * i, 128 * (i + 1))
        tops = []
        for e in range(2):
            score, mine = pair_scores(
                e, q_ref[:, pair], k_ref[:, pair], hot_own, hot_ref, b_ref[2 * i + e], mask
            )
            top = jnp.max(score, axis=1, keepdims=True)
            weight = jnp.exp(score - top).astype(bf16)
            acc_ref[2 * i + e] = dot_nn(weight, jnp.where(mine, v_ref[:, pair], bf16(1)))
            tops.append(top)
        top_ref[:, pair] = jnp.where(low, tops[0], tops[1])


def attn_far_kernel(
    d_ref, q_ref, k_ref, v_ref, hot_ref, hotq_ref, b_ref, acc_ref, top_ref, h0_ref, wout_ref, vec_ref,
    r1_ref, h1_ref, h1r_ref, ctx_s,
):
    rows = q_ref.shape[0]
    low = lane_low()
    mask = jnp.concatenate([place_mask(d_ref, rows, b, (1, rows), 1) for b in (2, 3)], axis=1)
    hot_own = hotq_ref[0:rows, :]
    for i in range(HEADS // 2):
        pair = slice(128 * i, 128 * (i + 1))
        outs = []
        for e in range(2):
            score, mine = pair_scores(
                e, q_ref[:, pair], k_ref[:, pair], hot_own, hot_ref, b_ref[2 * i + e], mask
            )
            old_top = top_ref[:, 128 * i + 64 * e : 128 * i + 64 * e + 1]
            top = jnp.maximum(jnp.max(score, axis=1, keepdims=True), old_top)
            weight = jnp.exp(score - top).astype(bf16)
            acc = dot_nn(weight, jnp.where(mine, v_ref[:, pair], bf16(1)))
            acc = acc + acc_ref[2 * i + e] * jnp.exp(old_top - top)
            outs.append(acc / pltpu.roll(acc, 64, 1))
        ctx_s[:, pair] = jnp.where(low, outs[0], outs[1]).astype(bf16)
    resid = h0_ref[...] + (dot_nn(ctx_s[...], wout_ref[...]) + vec_ref[0:1, :])
    r1_ref[...] = resid
    hidden = norm_parts(resid)[0] * vec_ref[1:2, :] + vec_ref[2:3, :]
    h1_ref[...] = hidden
    h1r_ref[...] = hidden.astype(bf16)


def attn_near(scalars, q, k, v, hot, bias):
    rows, width = q.shape
    return resident(
        attn_near_kernel, 5, 10, (scalars, q, k, v, hot, bias),
        [((HEADS, rows, 128), f32), ((rows, width), f32)],
    )


def attn_far(scalars, q, k, v, hot, hot_near, bias, acc, top, h0, w_out, vec):
    rows, width = q.shape
    return resident(
        attn_far_kernel, 7, 12,
        (scalars, q, k, v, hot, hot_near, bias, acc, top, h0, w_out, vec),
        [((rows, width), f32), ((rows, width), f32), ((rows, width), bf16)],
        [((rows, width), bf16)],
    )


def gelu_parts(u):
    phi = 0.5 + 0.5 * lax.erf(u * 0.7071067811865476)
    dens = jnp.exp(-0.5 * (u * u)) * 0.3989422804014327
    return u * phi, phi + u * dens


def norm_back(grad, xhat, rstd, gain):
    scaled = grad * gain
    mean_a = jnp.mean(scaled, axis=-1, keepdims=True)
    mean_b = jnp.mean(scaled * xhat, axis=-1, keepdims=True)
    return rstd * (scaled - mean_a - xhat * mean_b)


def col_sum(values):
    return jnp.sum(values, axis=0, keepdims=True)


def ffn_fwd_kernel(
    h1r_ref, wup_ref, bup_ref, wdown_ref, h1_ref, cot_ref, vec_ref,
    out_ref, dy_ref, dr2_ref, gp_ref, sums_ref,
):
    width = h1_ref.shape[1]
    h1r = h1r_ref[...]
    total = vec_ref[3:4, :]
    for c in range(0, wup_ref.shape[1], width):
        part = slice(c, c + width)
        g, slope = gelu_parts(dot_nn(h1r, wup_ref[:, part]) + bup_ref[0:1, part])
        gp_ref[:, part] = slope.astype(bf16)
        total = total + dot_nn(g.astype(bf16), wdown_ref[part, :])
    gain = vec_ref[4:5, :]
    xhat, rstd = norm_parts(h1_ref[...] + total)
    out_ref[0, 0] = (xhat * gain + vec_ref[5:6, :]).astype(bf16)
    grad = cot_ref[0, 0].astype(f32)
    dr2 = norm_back(grad, xhat, rstd, gain)
    dr2_ref[...] = dr2
    dy = dr2.astype(bf16)
    dy_ref[...] = dy
    sums_ref[0:1, :] = col_sum(dy.astype(f32))
    sums_ref[1:2, :] = col_sum(grad * xhat)
    sums_ref[2:3, :] = col_sum(grad)
    sums_ref[3:8, :] = jnp.zeros((5, width), f32)


def ffn_fwd(h1r, w_up, b_up, w_down, h1, cot, vec):
    rows, width = h1.shape
    return resident(
        ffn_fwd_kernel, 5, 14, (h1r, w_up, b_up, w_down, h1, cot, vec),
        [
            (cot.shape, bf16), ((rows, width), bf16), ((rows, width), f32),
            ((rows, w_up.shape[1]), bf16), ((8, width), f32),
        ],
        scalars=0,
    )


def ffn_bwd_kernel(
    dy_ref, wdown_ref, gp_ref, wup_ref, dr2_ref, r1_ref, vec_ref, dr1_ref, da_ref, sums_ref
):
    width = dr2_ref.shape[1]
    dy = dy_ref[...]
    grad = dr2_ref[...]
    for c in range(0, wup_ref.shape[1], width):
        part = slice(c, c + width)
        du = (dot_nt(dy, wdown_ref[part, :]) * gp_ref[:, part].astype(f32)).astype(bf16)
        grad = grad + dot_nt(du, wup_ref[:, part])
    xhat, rstd = norm_parts(r1_ref[...])
    dr1 = norm_back(grad, xhat, rstd, vec_ref[1:2, :])
    dr1_ref[...] = dr1
    da = dr1.astype(bf16)
    da_ref[...] = da
    sums_ref[0:1, :] = col_sum(da.astype(f32))
    sums_ref[1:2, :] = col_sum(grad * xhat)
    sums_ref[2:3, :] = col_sum(grad)
    sums_ref[3:4, :] = col_sum(dr1)
    sums_ref[4:8, :] = jnp.zeros((4, width), f32)


def ffn_bwd(dy, w_down, gp, w_up, dr2, r1, vec):
    rows, width = dr2.shape
    return resident(
        ffn_bwd_kernel, 3, 14, (dy, w_down, gp, w_up, dr2, r1, vec),
        [((rows, width), f32), ((rows, width), bf16), ((8, width), f32)],
        scalars=0,
    )


def ffn_again_kernel(d_ref, *refs):
    h1_refs, (wup_ref, bup_ref, g_ref, gp_ref) = refs[:4], refs[4:]
    rows = h1_refs[0].shape[0]
    part = g_ref.shape[1]
    cols = pl.ds(pl.multiple_of(d_ref[0] * part, 128), part)
    w_up = wup_ref[:, cols]
    b_up = bup_ref[0:1, cols]
    for b in range(4):
        g, slope = gelu_parts(dot_nn(h1_refs[b][...], w_up) + b_up)
        g_ref[b * rows : (b + 1) * rows, :] = g.astype(bf16)
        gp_ref[b * rows : (b + 1) * rows, :] = slope.astype(bf16)


def ffn_again(scalars, h1_blocks, w_up, b_up):
    rows = h1_blocks[0].shape[0]
    part = w_up.shape[1] // 4
    return resident(
        ffn_again_kernel, 3, 14, (scalars, *h1_blocks, w_up, b_up), [((4 * rows, part), bf16)] * 2
    )


def store_shares(bit, pieces, send_ref, keep_ref):
    half = len(pieces) // 2
    for mine in (0, 1):

        @pl.when(bit == mine)
        def _():
            for n, piece in enumerate(pieces):
                ref = keep_ref if n // half == mine else send_ref
                ref[n % half] = piece()


def owner_order(pages, bits):
    order = [0]
    for bit in reversed(bits):
        order = order + [o | (1 << bit) for o in order]
    count = len(bits)
    return [sum(((n >> (count - 1 - k)) & 1) << bit for k, bit in enumerate(bits)) for n in range(pages)]


def down_kernel(order, bit_ref, g_ref, ctx_ref, *refs):
    dy_refs, da_refs, (send_ref, keep_ref, dy_s, da_s, res_s) = refs[:4], refs[4:8], refs[8:]
    rows, width = dy_refs[0].shape
    for b in range(4):
        dy_s[b * rows : (b + 1) * rows, :] = dy_refs[b][...]
        da_s[b * rows : (b + 1) * rows, :] = da_refs[b][...]
    size = g_ref.shape[1]
    for n in range(0, size, 256):
        res_s[n : n + 256, :] = dot_tn(g_ref[:, n : n + 256], dy_s[...]).astype(bf16)
    res_s[size:, :] = dot_nn(ctx_ref[...], da_s[...]).astype(bf16)
    pages = len(order)
    down, out = size // pages, ctx_ref.shape[0] // pages

    def piece(owner):
        return lambda: jnp.concatenate(
            [
                res_s[owner * down : (owner + 1) * down, :].astype(f32),
                res_s[size + owner * out : size + (owner + 1) * out, :].astype(f32),
            ],
            axis=0,
        ).astype(bf16)

    store_shares(bit_ref[0], [piece(owner) for owner in order], send_ref, keep_ref)


def down_grad(bit, order, g_q, ctx_t, dy_blocks, da_blocks):
    rows, width = dy_blocks[0].shape
    size, out = g_q.shape[1], ctx_t.shape[0]
    pages = len(order)
    share = ((pages // 2, (size + out) // pages, width), bf16)
    return resident(
        functools.partial(down_kernel, order), 4, 16, (bit, g_q, ctx_t, *dy_blocks, *da_blocks),
        [share, share],
        [((4 * rows, width), bf16), ((4 * rows, width), bf16), ((size + out, width), bf16)],
    )


def up_kernel(order, d_ref, bit_ref, gp_ref, wdown_ref, *refs):
    dy_refs, h1_refs, (send_ref, keep_ref, sums_ref, du_s, h1_s, res_s) = refs[:4], refs[4:8], refs[8:]
    rows, width = dy_refs[0].shape
    size = gp_ref.shape[1]
    w_down = wdown_ref[pl.ds(pl.multiple_of(d_ref[0] * size, 128), size), :]
    for b in range(4):
        part = slice(b * rows, (b + 1) * rows)
        du = (dot_nt(dy_refs[b][...], w_down) * gp_ref[part, :].astype(f32)).astype(bf16)
        du_s[part, :] = du
        h1_s[part, :] = h1_refs[b][...]
        total = col_sum(du.astype(f32))
        sums = total if b == 0 else sums + total
    sums_ref[...] = jnp.broadcast_to(sums, sums_ref.shape)
    for n in range(0, width, 256):
        res_s[n : n + 256, :] = dot_tn(h1_s[:, n : n + 256], du_s[...])
    pages = len(order)
    own = width // 4
    rows = own // pages

    def piece(owner):
        starts = [q * own + owner * rows for q in (0, 2, 1, 3)]
        return lambda: jnp.stack([res_s[n : n + rows, :].astype(bf16) for n in starts])

    store_shares(bit_ref[0], [piece(owner) for owner in order], send_ref, keep_ref)


def up_grad(scalars, bit, order, gp_q, w_down, dy_blocks, h1_blocks):
    rows, width = dy_blocks[0].shape
    part = gp_q.shape[1]
    pages = len(order)
    share = ((pages // 2, 4, width // 4 // pages, part), bf16)
    return resident(
        functools.partial(up_kernel, order), 3.5, 20,
        (scalars, bit, gp_q, w_down, *dy_blocks, *h1_blocks),
        [share, share, ((8, part), f32)],
        [((4 * rows, part), bf16), ((4 * rows, width), bf16), ((width, part), f32)], scalars=2,
    )


def step_kernel(bit_ref, keep_ref, got_ref, *out_refs):
    half = keep_ref.shape[0] // 2
    for ref, bit in zip(out_refs, (1 - bit_ref[0], bit_ref[0])):
        part = pl.ds(bit * half, half)
        ref[...] = (keep_ref[part].astype(f32) + got_ref[part].astype(f32)).astype(bf16)


def add_kernel(bit_ref, keep_ref, got_ref, out_ref):
    out_ref[...] = (keep_ref[...].astype(f32) + got_ref[...].astype(f32)).astype(bf16)


def step_sum(bit, keep, got):
    if keep.shape[0] == 1:
        return resident(add_kernel, 0.5, 6, (bit, keep, got), [(keep.shape, bf16)])[0]
    half = (keep.shape[0] // 2,) + keep.shape[1:]
    return resident(step_kernel, 0.7, 8, (bit, keep, got), [(half, bf16)] * 2)


def weights_kernel(
    d_ref, h0a_ref, h0b_ref, warr_ref, barr_ref, hota_ref, hotb_ref, b_ref,
    p_ref, kat_ref, et_ref, r_ref, ctx_ref, h0t_ref,
):
    rows = h0a_ref.shape[0] // 2
    half = 2 * rows
    own = HEADS // 4
    low = lane_low()
    one = jnp.ones((), bf16)
    mask = jnp.concatenate([place_mask(d_ref, rows, b, (1, rows), 1) for b in range(4)], axis=1)
    hots = (hota_ref, hotb_ref)
    for n, ref in enumerate((h0a_ref, h0b_ref)):
        part = slice(half * n, half * (n + 1))
        p_ref[part, :] = (dot_nn(ref[...], warr_ref[...]) + barr_ref[0:1, :]).astype(bf16)
        h0t_ref[:, part] = ref[...].T
    for j in range(own):
        kv = p_ref[:, 256 * j : 256 * j + 128]
        hot = jnp.concatenate([hota_ref[...], hotb_ref[...]], axis=0)
        k_aug = jnp.concatenate([jnp.where(low, kv, hot[:, 0:128]), hot[:, 128:256]], axis=1)
        kat_ref[j] = k_aug.T
        v_one_t = jnp.where(low, one, kv).T
        bias = b_ref[d_ref[0] * own + j]
        for block in range(4):
            part = slice(rows * block, rows * (block + 1))
            hot_q = hots[block // 2][rows * (block % 2) : rows * (block % 2 + 1), :]
            q_only = p_ref[part, 256 * j + 128 : 256 * j + 256] * bf16(0.125)
            side = dot_nn(hot_q, bias).astype(bf16)
            q_aug = jnp.concatenate([jnp.where(low, q_only, side[:, 0:128]), side[:, 128:256]], axis=1)
            score = dot_nt(q_aug, k_aug) + mask
            top = jnp.max(score, axis=1, keepdims=True)
            weight = jnp.exp(score - top).astype(bf16)
            et_ref[j, :, part] = weight.T
            acc = dot_nt(v_one_t, weight)
            recip = 1.0 / acc[0:8, :]
            r_ref[8 * j : 8 * (j + 1), part] = recip
            ctx_ref[64 * j : 64 * (j + 1), part] = (acc[64:128, :] * recip[0:1, :]).astype(bf16)


def own_weights(scalars, h0_near, h0_far, w_arr, b_arr, hot_near, hot_far, bias):
    keys = 2 * h0_near.shape[0]
    width = h0_near.shape[1]
    own = HEADS // 4
    return resident(
        weights_kernel, 11, 16,
        (scalars, h0_near, h0_far, w_arr, b_arr, hot_near, hot_far, bias),
        [
            ((keys, width), bf16), ((own, 256, keys), bf16), ((own, keys, keys), bf16),
            ((own * 8, keys), f32), ((own * 64, keys), bf16), ((width, keys), bf16),
        ],
    )


def attn_bwd_kernel(head, h0t_ref, *refs):
    da_refs = refs[:4]
    p_ref, kat_ref, et_ref, r_ref, warr_ref, oarr_ref, hota_ref, hotb_ref = refs[4:12]
    dp_ref, dw_ref, tab_ref, row_ref = refs[12:]
    rows, width = da_refs[0].shape
    keys = 4 * rows
    low = lane_low()
    zero = jnp.zeros((), bf16)
    cols = slice(256 * head, 256 * (head + 1))
    v_only = jnp.where(low, zero, p_ref[:, 256 * head : 256 * head + 128])
    k_aug_t = kat_ref[head]
    oarr = oarr_ref[128 * head : 128 * (head + 1), :]
    w_arr = warr_ref[:, cols]
    hots = (hota_ref, hotb_ref)
    acc_kv = jnp.zeros((keys, 128), f32)
    acc_b = jnp.zeros((256, 256), f32)
    for block in range(4):
        part = slice(rows * block, rows * (block + 1))
        q_only = p_ref[part, 256 * head + 128 : 256 * head + 256] * bf16(0.125)
        hot_q = hots[block // 2][rows * (block % 2) : rows * (block % 2 + 1), :]
        recip = r_ref[8 * head : 8 * (head + 1), part]
        dc = (dot_nt(da_refs[block][...], oarr) * recip.T[:, 0:1]).astype(bf16)
        weight_low = et_ref[head, :, part]
        weight = weight_low.astype(f32)
        dweight = dot_nt(v_only, dc)
        inner = jnp.sum(weight * dweight, axis=0, keepdims=True) * recip[0:1, :]
        dscore = (weight * (dweight - inner)).astype(bf16)
        acc_kv = acc_kv + (dot_nn(dscore, q_only) + dot_nn(weight_low, dc))
        dq_aug_t = dot_nn(k_aug_t, dscore)
        dq = dq_aug_t[0:128, :].T * 0.125
        dp_ref[part, 128:256] = jnp.where(low, dq, 0.0).astype(bf16)
        acc_b = acc_b + dot_nn(dq_aug_t.astype(bf16), hot_q)
    dp_ref[:, 0:128] = acc_kv.astype(bf16)
    dp = dp_ref[...]
    dw_ref[...] = dot_nn(h0t_ref[...], dp)
    total = col_sum(dp.astype(f32))
    row_ref[...] = jnp.zeros(row_ref.shape, f32)
    row_ref[0:1, 0:256] = total
    high = total.astype(bf16)
    rest = (total - high.astype(f32)).astype(bf16)
    lang = dot_nt(jnp.broadcast_to(high, (8, 256)), w_arr)
    lang = lang + dot_nt(jnp.broadcast_to(rest, (8, 256)), w_arr)
    row_ref[1:2, :] = lang[0:1, :]
    for first, block in (
        (0, acc_b[64:96, 0:128]), (32, acc_b[96:128, 0:128]), (64, acc_b[128:256, 128:256]),
    ):
        size = block.shape[0]
        lane = iota((size, 128), 1)
        key = iota((size, 128), 0)
        if first == 32:
            lane = lane - 32
        index = jnp.clip(key - lane, -16, 15) + 16
        if size == 32:
            index = jnp.where(jnp.logical_and(lane >= 0, lane < 32), index, -1)
        for bucket in range(32):
            at = first + bucket
            tab_ref[at : at + 1, :] = col_sum(jnp.where(index == bucket, block, 0.0))


def attn_bwd(head, h0_t, da_blocks, p_all, kat, et, recip, w_arr, o_arr, hot_near, hot_far):
    rows, width = da_blocks[0].shape
    keys = 4 * rows
    return resident(
        functools.partial(attn_bwd_kernel, head), 6, 12,
        (h0_t, *da_blocks, p_all, kat, et, recip, w_arr, o_arr, hot_near, hot_far),
        [((keys, 256), bf16), ((width, 256), f32), ((96, 128), f32), ((8, width), f32)],
        scalars=0,
    )


def input_kernel(*refs):
    dp_refs, (warr_ref, dr1_ref, own_ref, near_ref, far_ref) = refs[:3], refs[3:]
    rows = dr1_ref.shape[0]
    dp = jnp.concatenate([ref[...] for ref in dp_refs], axis=1)
    for b in (1, 3, 2, 0):
        part = dot_nt(dp[b * rows : (b + 1) * rows, :], warr_ref[...])
        if b == 0:
            own_ref[...] = dr1_ref[...] + part
        elif b == 2:
            far_ref[...] = part
        else:
            near_ref[(b // 2) * rows : (b // 2 + 1) * rows, :] = part.astype(bf16)


def input_parts(dps, w_arr, dr1):
    rows, width = dr1.shape
    return resident(
        input_kernel, 1.5, 12, (*dps, w_arr, dr1),
        [((rows, width), f32), ((2 * rows, width), bf16), ((rows, width), f32)], scalars=0,
    )


SMALL_ROWS = 96


def pack_kernel(pages, d_ref, *refs):
    one_ref, two_ref, up_ref = refs[:3]
    dw_refs, row_refs, tab_refs, (out_ref, m_s) = refs[3:6], refs[6:9], refs[9:12], refs[12:]
    quarter, language = d_ref[0], d_ref[2]
    width = one_ref.shape[1]
    own = HEADS // 4
    cols = own * 64
    n = cols // pages
    m_s[...] = jnp.zeros(m_s.shape, f32)
    lang = one_ref[3:4, :]
    for ref in row_refs:
        lang = lang + ref[1:2, :]
    vectors = [one_ref[k : k + 1, :] for k in range(3)] + [two_ref[k : k + 1, :] for k in range(3)]
    vectors += [None, None, None, None, None, None]
    vectors += [jnp.where(language == k, lang, 0.0) for k in range(7)]
    lane = iota((32, 128), 1)
    tables = [jnp.zeros((32, 128), f32) for _ in range(3)]
    for j in range(own):
        sums = jnp.sum(tab_refs[j][...], axis=1, keepdims=True)
        for t in range(3):
            at = 12 * t + quarter * own + j
            tables[t] = jnp.where(lane == at, sums[32 * t : 32 * (t + 1), :], tables[t])
    table = tables[0] + tables[1] + tables[2]
    for q in range(4):
        mine = quarter == q
        for k, vector in enumerate(vectors):
            if vector is not None:
                for part in range(own):
                    first = q * cols + 64 * part
                    m_s[q, 3 * k + part : 3 * k + part + 1, 0:64] = vector[:, first : first + 64]
        for j in range(own):
            row = row_refs[j]
            m_s[q, 18 + j : 19 + j, 0:64] = jnp.where(mine, row[0:1, 128:192], 0.0)
            m_s[q, 21 + j : 22 + j, 0:64] = jnp.where(mine, row[0:1, 64:128], 0.0)
        for k in range(12):
            m_s[q, 24 + k : 25 + k, 0:64] = jnp.where(mine, up_ref[0:1, 64 * k : 64 * (k + 1)], 0.0)
        m_s[q, 64:72, 0:64] = table[8 * q : 8 * (q + 1), 0:64]
    share = SMALL_ROWS // pages
    zeros = jnp.zeros((n - share, 64), f32)
    for q in range(4):
        for p in range(pages):
            first = q * cols + p * n
            pieces = [ref[first : first + n, 64 * t : 64 * (t + 1)] for t in range(3) for ref in dw_refs]
            small = m_s[q, p * share : (p + 1) * share, 0:64]
            pieces.append(jnp.concatenate([small, zeros], axis=0))
            out_ref[p * 4 + q] = jnp.concatenate(pieces, axis=1).astype(bf16)


def pack(scalars, pages, sums_one, sums_two, sums_up, dws, rows_out, tabs):
    n = dws[0].shape[0] // 4 // pages
    return resident(
        functools.partial(pack_kernel, pages), 2, 12,
        (scalars, sums_one, sums_two, sums_up, *dws, *rows_out, *tabs),
        [((4 * pages, n, 640), bf16)], [((4, SMALL_ROWS, 128), f32)],
    )[0]


def gather_kernel(got_ref, out_ref):
    pages = got_ref.shape[0] // 4
    small = None
    for q in range(4):
        total = got_ref[q].astype(f32)
        for p in range(1, pages):
            total = total + got_ref[4 * p + q].astype(f32)
        out_ref[q] = total.astype(bf16)
        part = total[:, 576:640]
        small = part if small is None else small + part
    for q in range(4):
        out_ref[q, :, 576:640] = small.astype(bf16)


def gather_sum(got):
    return resident(gather_kernel, 1, 8, (got,), [((4,) + got.shape[1:], bf16)], scalars=0)[0]


def heads_kernel(got_ref, key_ref, value_ref, query_ref, vec_ref, lang_ref, tab_ref, m_s):
    pages, _, n, _ = got_ref.shape
    share = SMALL_ROWS // pages
    for p in range(pages):
        blocks = [got_ref[p, q].astype(f32) for q in range(4)]
        for t, ref in enumerate((key_ref, value_ref, query_ref)):
            ref[p * n : (p + 1) * n, :] = jnp.concatenate(
                [block[:, 192 * t : 192 * (t + 1)] for block in blocks], axis=1
            )
        m_s[p * share : (p + 1) * share, 0:64] = blocks[0][0:share, 576:640]
    vec_ref[...] = jnp.zeros(vec_ref.shape, f32)
    for k in range(8):
        for part in range(3):
            vec_ref[k : k + 1, 64 * part : 64 * (part + 1)] = m_s[3 * k + part : 3 * k + part + 1, 0:64]
    for k in range(12):
        vec_ref[8:9, 64 * k : 64 * (k + 1)] = m_s[24 + k : 25 + k, 0:64]
    for part in range(3):
        piece = jnp.concatenate(
            [m_s[36 + 3 * k + part : 37 + 3 * k + part, 0:64] for k in range(7)] + [jnp.zeros((1, 64), f32)], axis=0
        )
        lang_ref[64 * part : 64 * (part + 1), :] = piece.T[:, 0:7]
    for t in range(3):
        tab_ref[t] = m_s[64:72, 12 * t : 12 * (t + 1)]


def finish_heads(got):
    pages, _, n, _ = got.shape
    rows = pages * n
    mat = ((rows, 4 * rows), f32)
    return resident(
        heads_kernel, 3, 12, (got,),
        [mat, mat, mat, ((16, 768), f32), ((rows, 7), f32), ((3, 8, HEADS), f32)],
        [((SMALL_ROWS, 128), f32)], scalars=0,
    )


def up_finish_kernel(distances, d_ref, got_ref, out_ref):
    pages, _, n, part = got_ref.shape
    for p, distance in enumerate(distances):
        for q in range(4):
            cols = pl.ds(pl.multiple_of((d_ref[0] ^ q) * part, 128), part)
            out_ref[d_ref[3] ^ distance, :, cols] = got_ref[p, q].astype(f32)


def finish_up(scalars, got, distances):
    pages, _, n, part = got.shape
    kernel = functools.partial(up_finish_kernel, distances)
    rows = resident(kernel, 2, 8, (scalars, got), [((pages, n, 4 * part), f32)])[0]
    return rows.reshape(pages * n, 4 * part)


def down_finish_kernel(distances, d_ref, got_ref, down_ref, out_ref):
    down = down_ref.shape[1]
    for p, distance in enumerate(distances):
        owner = d_ref[3] ^ distance
        block = got_ref[p].astype(f32)
        down_ref[owner] = block[0:down, :]
        out_ref[owner] = block[down:, :]


def finish_down(scalars, got, size, out, distances):
    pages, _, width = got.shape
    kernel = functools.partial(down_finish_kernel, distances)
    blocks = resident(
        kernel, 2, 8, (scalars, got),
        [((pages, size // pages, width), f32), ((pages, out // pages, width), f32)],
    )
    return blocks[0].reshape(size, width), blocks[1].reshape(out, width)


def swap(values, axis, bit=0):
    size = lax.axis_size(axis)
    return lax.ppermute(values, axis, [(i, i ^ (1 << bit)) for i in range(size)])


def page_gather(own):
    near = swap(own, "seq")
    far = swap(own, "stream")
    return [own, near, far, swap(far, "seq")]


def page_bit(bit):
    return ((lax.axis_index("page") >> bit) & 1).astype(i32).reshape(1)


def exchange_kernel(bit_ref, x_ref, send_ref, keep_ref):
    send_ref[...] = x_ref[1 - bit_ref[0]]
    keep_ref[...] = x_ref[bit_ref[0]]


def turn_near(own, axis_bit):
    shape = own.shape[1:]
    return resident(exchange_kernel, 0.5, 6, (axis_bit, own), [(shape, bf16)] * 2)


def turn_far_kernel(bit_ref, keep_ref, got_ref, send_ref, stay_ref):
    for ref, at in ((send_ref, 1 - bit_ref[0]), (stay_ref, bit_ref[0])):
        ref[0] = keep_ref[at]
        ref[1] = got_ref[at]


def turn_far(keep, got, axis_bit):
    shape = (2,) + keep.shape[1:]
    return resident(turn_far_kernel, 0.5, 6, (axis_bit, keep, got), [(shape, bf16)] * 2)


def page_swap(values, bit):
    return swap(values, "page", bit)


def on_device(
    tokens, boxes, text_lengths, language, lang_table, w_query, b_query, w_key, w_value, b_value,
    w_out, b_out, norm1_gain, norm1_bias, w_up, b_up, w_down, b_down, norm2_gain, norm2_bias,
    table_pos, table_x, table_y, cotangent,
):
    rows = tokens.shape[2]
    width = tokens.shape[3]
    head_dim = width // HEADS
    own_heads = HEADS // 4
    own_cols = own_heads * head_dim
    pages = lax.axis_size("page")
    count = pages.bit_length() - 1
    page = lax.axis_index("page").astype(i32)
    stream = lax.axis_index("stream").astype(i32).reshape(1)
    seq = lax.axis_index("seq").astype(i32).reshape(1)
    quarter = lax.axis_index(("stream", "seq")).astype(i32)
    scalars = jnp.concatenate([quarter.reshape(1), text_lengths, language, page.reshape(1)])

    h0, message = prep(language, tokens, boxes.reshape(2, 1, 1, rows), lang_table)
    own_msg, near_msg, far_msg, last_msg = page_gather(message)

    vec = jnp.concatenate(
        [b_out, norm1_gain, norm1_bias, b_down, norm2_gain, norm2_bias, b_query, b_value]
    )
    vec = vec.reshape(8, width).astype(f32)
    b_up_row = b_up[None, :].astype(f32)
    bias = bias_mats(table_x, table_y, table_pos)

    k_near, v_near, hot_near, h0_near, q_own = project(
        scalars, own_msg, near_msg, w_key, w_value, vec, 0, w_query
    )
    acc, top = attn_near(scalars, q_own, k_near, v_near, hot_near, bias)
    far_msg, last_msg = after((far_msg, last_msg), acc)
    k_far, v_far, hot_far, h0_far = project(scalars, far_msg, last_msg, w_key, w_value, vec, 2)
    r1, h1, h1r = attn_far(
        scalars, q_own, k_far, v_far, hot_far, hot_near, bias, acc, top, h0, w_out, vec
    )
    h1_blocks = page_gather(h1r)
    layer_out, dy, dr2, gp, sums_two = ffn_fwd(h1r, w_up, b_up_row, w_down, h1, cotangent, vec)
    dy_near, dy_far = swap(dy, "seq"), swap(dy, "stream")
    dr1, da, sums_one = ffn_bwd(dy, w_down, gp, w_up, dr2, r1, vec)
    da_near, da_far = swap(da, "seq"), swap(da, "stream")

    w_arr, b_arr, o_arr = pick_weights(after(scalars, acc), w_key, w_value, w_query, vec, w_out)
    p_all, kat, pt, recip, ctx_t, h0_t = own_weights(
        after(scalars, da), h0_near, h0_far, w_arr, b_arr, hot_near, hot_far, bias
    )
    dy_far = after(dy_far, pt)
    dy_blocks = [dy, dy_near, dy_far, swap(dy_far, "seq")]
    g_q, gp_q = ffn_again(after(scalars, pt), h1_blocks, w_up, b_up_row)

    up_bits = list(range(count))
    down_bits = list(range(count))
    up_send, up_keep, sums_up = up_grad(
        scalars, page_bit(up_bits[0]), owner_order(pages, up_bits), gp_q, w_down, dy_blocks, h1_blocks
    )
    up_got = page_swap(up_send, up_bits[0])
    da_far = after(da_far, up_keep)
    da_blocks = [da, da_near, da_far, swap(da_far, "seq")]
    down_send, down_keep = down_grad(
        page_bit(down_bits[0]), owner_order(pages, down_bits), g_q, ctx_t, dy_blocks, da_blocks
    )
    down_got = page_swap(down_send, down_bits[0])

    state = {"up": (up_keep, up_got, 0), "down": (down_keep, down_got, 0)}
    bits_of = {"up": up_bits, "down": down_bits}

    def advance(name):
        keep, got, at = state[name]
        at += 1
        if at < count:
            send, keep = step_sum(page_bit(bits_of[name][at]), keep, got)
            state[name] = (keep, page_swap(send, bits_of[name][at]), at)
        else:
            state[name] = (step_sum(page_bit(0), keep, got), None, at)

    def backward(j, order_on=()):
        return attn_bwd(
            j, h0_t, da_blocks, p_all, kat, after(pt, *order_on), recip, w_arr, o_arr, hot_near, hot_far
        )

    heads = [backward(0, (down_keep,))]
    heads.append(backward(1, (heads[0][0],)))
    heads.append(backward(2, (heads[1][0],)))
    dps, dws, tabs, rows_out = zip(*heads)

    packed = pack(scalars, pages, sums_one, sums_two, sums_up, dws, rows_out, tabs)
    got_heads = lax.all_to_all(packed, PAGE_AXES, 0, 0)

    own_part, near_part, far_part = input_parts(dps, w_arr, dr1)
    got_near = swap(near_part, "seq").astype(f32)
    got_far = swap((far_part + got_near[rows:]).astype(bf16), "stream").astype(f32)
    input_grad = ((own_part + got_near[:rows]) + got_far).astype(bf16)

    for _ in range(count):
        advance("up")
        advance("down")

    share = state["up"][0][0]
    share = share.reshape((2, 2) + share.shape[1:])
    send, keep = turn_near(share, seq)
    send, keep = turn_far(keep, swap(send, "seq"), stream)
    up_mine = jnp.concatenate([keep, swap(send, "stream")], axis=0)[None]
    down_mine = state["down"][0]
    for bit in range(count - 1, -1, -1):
        up_mine = jnp.concatenate([up_mine, page_swap(up_mine, bit)], axis=0)
        down_mine = jnp.concatenate([down_mine, page_swap(down_mine, bit)], axis=0)
    by_distance = [
        sum(((n >> k) & 1) << (count - 1 - k) for k in range(count)) for n in range(pages)
    ]
    res_up = finish_up(scalars, up_mine, tuple(by_distance))
    part = w_up.shape[1] // 4
    res_down, res_out = finish_down(scalars, down_mine, part, own_cols, tuple(by_distance))

    mine_heads = gather_sum(got_heads)
    all_heads = lax.all_to_all(
        jnp.broadcast_to(mine_heads[None], (pages,) + mine_heads.shape), "page", 0, 0
    )
    res_key, res_value, res_query, vecs, s_lang, s_tab = finish_heads(all_heads)
    s_bout, s_g1, s_s1, s_bdown, s_g2, s_s2, s_bq, s_bv = (vecs[i, :own_cols] for i in range(8))
    return (
        layer_out, input_grad[None, None], s_lang, res_query, s_bq, res_key, res_value, s_bv,
        res_out, s_bout, s_g1, s_s1, res_up, vecs[8], res_down, s_bdown, s_g2, s_s2,
        s_tab[2], s_tab[0], s_tab[1],
    )


def solution(mesh):
    token_spec = P("page", "stream", "seq", None)
    rep = P()
    in_specs = (
        (token_spec, P(None, "page", "stream", "seq"), P("page"), P("page"))
        + (rep,) * 19
        + (token_spec,)
    )
    mat, vec = P(("stream", "seq"), None), P(("stream", "seq"))
    out_specs = (
        token_spec, token_spec, mat, mat, vec, mat, mat, vec, mat, vec, vec, vec,
        mat, vec, mat, vec, vec, vec, mat, mat, mat,
    )
    return jax.shard_map(
        on_device, mesh=mesh, in_specs=in_specs, out_specs=out_specs, check_vma=False
    )
```

```python
import functools

import jax
import jax.numpy as jnp
import numpy as np
from jax import lax
from jax.experimental import pallas as pl
from jax.experimental.pallas import tpu as pltpu
from jax.sharding import PartitionSpec as P

HEADS = 12
BOX_ROWS = 16
norm_eps = 1e-05
masked_score = -1000000000.0
level_step = 8
f32 = jnp.float32
bf16 = jnp.bfloat16
i32 = jnp.int32
MB = 1 << 20
SCOPED_MB = 12
PAGE_AXES = ("page", "stream", "seq")


def dot_nn(left, right):
    return lax.dot_general(left, right, (((1,), (0,)), ((), ())), preferred_element_type=f32)


def dot_nt(left, right):
    return lax.dot_general(left, right, (((1,), (1,)), ((), ())), preferred_element_type=f32)


def dot_tn(left, right):
    return lax.dot_general(left, right, (((0,), (0,)), ((), ())), preferred_element_type=f32)


def params(vmem_mb):
    return pltpu.CompilerParams(
        vmem_limit_bytes=vmem_mb * MB, dimension_semantics=("arbitrary",)
    )


def struct(shape, kind):
    return jax.ShapeDtypeStruct(shape, kind)


def whole(shape):
    return pl.BlockSpec(shape, lambda *at: (0,) * len(shape))


def fixed(shape, at):
    return pl.BlockSpec(shape, lambda *_: at)


def iota(shape, dim):
    return lax.broadcasted_iota(i32, shape, dim)


def lane_low():
    return iota((1, 128), 1) < 64


SMEM = pl.BlockSpec(memory_space=pltpu.SMEM)
VMEM = pl.BlockSpec(memory_space=pltpu.VMEM)


def cost(micros):
    return pl.CostEstimate(
        flops=int(micros * 1.15e10), bytes_accessed=int(micros * 3.69e7), transcendentals=0
    )


def resident(kernel, micros, args, outs, scratch=(), scalars=1):
    return pl.pallas_call(
        kernel,
        cost_estimate=cost(micros),
        in_specs=[SMEM] * scalars + [VMEM] * (len(args) - scalars),
        out_specs=[VMEM] * len(outs),
        out_shape=[struct(*out) for out in outs],
        scratch_shapes=[pltpu.VMEM(*entry) for entry in scratch],
        compiler_params=pltpu.CompilerParams(vmem_limit_bytes=SCOPED_MB * MB),
    )(*args)


def after(values, *others):
    return lax.optimization_barrier((values, others))[0]


def prep_kernel(lang_ref, tok_ref, box_ref, table_ref, h0_ref, msg_ref):
    rows, width = h0_ref.shape
    pick = (iota((8, table_ref.shape[0]), 1) == lang_ref[0]).astype(bf16)
    column = dot_nn(pick, table_ref[...])[0:1, :]
    h0 = tok_ref[0, 0].astype(f32) + column
    h0_ref[...] = h0
    msg_ref[0:rows, :] = h0.astype(bf16)
    row = iota((BOX_ROWS, rows), 0)
    box_x = jnp.broadcast_to(box_ref[0, 0], (BOX_ROWS, rows)).astype(f32)
    box_y = jnp.broadcast_to(box_ref[1, 0], (BOX_ROWS, rows)).astype(f32)
    packed = jnp.where(row == 0, box_x, jnp.where(row == 1, box_y, 0.0)).astype(bf16)
    msg_ref[rows : rows + BOX_ROWS, :] = jnp.zeros((BOX_ROWS, width), bf16)
    msg_ref[rows : rows + BOX_ROWS, 0:rows] = packed


def prep(language, tokens, boxes, lang_table):
    rows, width = tokens.shape[2:]
    return pl.pallas_call(
        prep_kernel,
        cost_estimate=cost(1),
        grid=(1,),
        in_specs=[SMEM, whole(tokens.shape), whole(boxes.shape), whole(lang_table.shape)],
        out_specs=[whole((rows, width)), whole((rows + BOX_ROWS, width))],
        out_shape=[struct((rows, width), f32), struct((rows + BOX_ROWS, width), bf16)],
        compiler_params=params(SCOPED_MB),
    )(language, tokens, boxes, lang_table)


def bias_kernel(tx_ref, ty_ref, tp_ref, out_ref):
    bucket = jnp.clip(iota((32, 256), 1) - 128, -16, 15) + 16
    marks = (bucket == iota((32, 256), 0)).astype(bf16)
    diag = [dot_nn(ref[...], marks) for ref in (tx_ref, ty_ref, tp_ref)]
    lane = iota((32, 128), 1)

    def shifted(row, rows):
        return pltpu.roll(jnp.broadcast_to(row, (rows, 256)), 0, 1, stride=1, stride_axis=0)[:, 128:256]

    out_ref[...] = jnp.zeros(out_ref.shape, bf16)
    for head in range(HEADS):
        x = jnp.where(lane < 32, shifted(diag[0][head : head + 1, :], 32), 0.0)
        y = jnp.where(lane < 32, shifted(diag[1][head : head + 1, :], 32), 0.0)
        out_ref[head, 0:32, 0:128] = (x + pltpu.roll(x, 64, 1)).astype(bf16)
        out_ref[head, 32:64, 0:128] = (pltpu.roll(y, 32, 1) + pltpu.roll(y, 96, 1)).astype(bf16)
        out_ref[head, 128:256, 128:256] = shifted(diag[2][head : head + 1, :], 128).astype(bf16)


def bias_mats(table_x, table_y, table_pos):
    return resident(
        bias_kernel, 2, (table_x, table_y, table_pos), [((HEADS, 256, 256), bf16)], scalars=0
    )[0]


def pick_kernel(d_ref, wk_ref, wv_ref, wq_ref, vec_ref, wo_ref, warr_ref, barr_ref, oarr_ref):
    head = d_ref[0] * (HEADS // 4) + pl.program_id(0)
    even = (head % 2) == 0
    low = lane_low()

    def arrange(k, v, q):
        k_low = jnp.where(even, k, pltpu.roll(k, 64, 1))
        v_high = jnp.where(even, pltpu.roll(v, 64, 1), v)
        q_low = jnp.where(even, q, pltpu.roll(q, 64, 1))
        return jnp.concatenate([jnp.where(low, k_low, v_high), jnp.where(low, q_low, 0.0)], axis=1)

    warr_ref[...] = arrange(
        wk_ref[...].astype(f32), wv_ref[...].astype(f32), wq_ref[...].astype(f32)
    ).astype(bf16)
    bv = jnp.broadcast_to(vec_ref[7:8, :], (8, 128))
    bq = jnp.broadcast_to(vec_ref[6:7, :], (8, 128))
    barr_ref[...] = arrange(jnp.zeros_like(bv), bv, bq)
    oarr_ref[0:64, :] = jnp.zeros((64, oarr_ref.shape[1]), bf16)
    oarr_ref[64:128, :] = wo_ref[...]


def pick_weights(scalars, w_key, w_value, w_query, vec, w_out):
    width = w_key.shape[0]
    own = HEADS // 4
    pair = lambda i, d: (0, (d[0] * own + i) // 2)
    return pl.pallas_call(
        pick_kernel,
        cost_estimate=cost(2),
        grid_spec=pltpu.PrefetchScalarGridSpec(
            num_scalar_prefetch=1,
            grid=(own,),
            in_specs=[pl.BlockSpec((width, 128), pair)] * 3
            + [pl.BlockSpec((8, 128), pair)]
            + [pl.BlockSpec((64, width), lambda i, d: (d[0] * own + i, 0))],
            out_specs=[
                pl.BlockSpec((width, 256), lambda i, d: (0, i)),
                pl.BlockSpec((8, 256), lambda i, d: (0, i)),
                pl.BlockSpec((128, width), lambda i, d: (i, 0)),
            ],
        ),
        out_shape=[
            struct((width, own * 256), bf16),
            struct((8, own * 256), f32),
            struct((own * 128, width), bf16),
        ],
        compiler_params=params(SCOPED_MB),
    )(scalars, w_key, w_value, w_query, vec, w_out)


def proj_kernel(with_query, first, d_ref, a_ref, b_ref, wk_ref, wv_ref, vec_ref, *refs):
    if with_query:
        wq_ref, k_ref, v_ref, hot_ref, h0_ref, q_ref = refs
    else:
        k_ref, v_ref, hot_ref, h0_ref = refs
    rows = a_ref.shape[0] - BOX_ROWS
    lane = iota((rows, 256), 1)
    for n, ref in enumerate((a_ref, b_ref)):
        h0_ref[n * rows : (n + 1) * rows, :] = ref[0:rows, :]
        boxes = ref[rows : rows + BOX_ROWS, 0:rows].astype(f32).T
        level = jnp.floor(boxes * (1.0 / level_step)).astype(i32)
        start = (d_ref[0] ^ (first + n)) * rows
        place = (start + iota((rows, 256), 0)) // level_step + 128
        flat = jnp.where(lane % 64 < 32, level[:, 0:1], level[:, 1:2] + 32) + (lane // 64) * 64
        want = jnp.where(lane >= 128, place, flat)
        hot_ref[n * rows : (n + 1) * rows, :] = (want == lane).astype(bf16)
    h0 = h0_ref[...]
    width = h0.shape[1]
    for c in range(0, width, 256):
        part = slice(c, c + 256)
        k_ref[:, part] = dot_nn(h0, wk_ref[:, part]).astype(bf16)
        v_ref[:, part] = (dot_nn(h0, wv_ref[:, part]) + vec_ref[7:8, part]).astype(bf16)
        if with_query:
            query = dot_nn(h0[0:rows, :], wq_ref[:, part]) + vec_ref[6:7, part]
            q_ref[:, part] = query.astype(bf16) * bf16(0.125)


def project(scalars, msg_a, msg_b, w_key, w_value, vec, first, w_query=None):
    rows = msg_a.shape[0] - BOX_ROWS
    width = msg_a.shape[1]
    keys = 2 * rows
    args = [scalars, msg_a, msg_b, w_key, w_value, vec]
    outs = [((keys, width), bf16), ((keys, width), bf16), ((keys, 256), bf16), ((keys, width), bf16)]
    if w_query is not None:
        args.append(w_query)
        outs.append(((rows, width), bf16))
    kernel = functools.partial(proj_kernel, w_query is not None, first)
    return resident(kernel, 2, args, outs)


def norm_parts(resid):
    center = resid - jnp.mean(resid, axis=-1, keepdims=True)
    spread = jnp.mean(center * center, axis=-1, keepdims=True)
    rstd = lax.rsqrt(spread + norm_eps)
    return center * rstd, rstd


def place_mask(d_ref, rows, first, shape, dim):
    place = (d_ref[0] ^ first) * rows + iota(shape, dim)
    live = jnp.logical_or(place >= 2 * rows, place < d_ref[1])
    return jnp.where(live, 0.0, masked_score).astype(f32)


def pair_scores(e, q_pair, k_pair, hot_own, hot_ref, bias, mask):
    low = lane_low()
    mine = low if e == 0 else jnp.logical_not(low)
    side = dot_nn(hot_own, bias).astype(bf16)
    q_aug = jnp.concatenate([jnp.where(mine, q_pair, side[:, 0:128]), side[:, 128:256]], axis=1)
    k_aug = jnp.concatenate([jnp.where(mine, k_pair, hot_ref[:, 0:128]), hot_ref[:, 128:256]], axis=1)
    return dot_nt(q_aug, k_aug) + mask, mine


def attn_near_kernel(d_ref, q_ref, k_ref, v_ref, hot_ref, b_ref, acc_ref, top_ref):
    rows = q_ref.shape[0]
    low = lane_low()
    mask = jnp.concatenate([place_mask(d_ref, rows, b, (1, rows), 1) for b in (0, 1)], axis=1)
    hot_own = hot_ref[0:rows, :]
    for i in range(HEADS // 2):
        pair = slice(128 * i, 128 * (i + 1))
        tops = []
        for e in range(2):
            score, mine = pair_scores(
                e, q_ref[:, pair], k_ref[:, pair], hot_own, hot_ref, b_ref[2 * i + e], mask
            )
            top = jnp.max(score, axis=1, keepdims=True)
            weight = jnp.exp(score - top).astype(bf16)
            acc_ref[2 * i + e] = dot_nn(weight, jnp.where(mine, v_ref[:, pair], bf16(1)))
            tops.append(top)
        top_ref[:, pair] = jnp.where(low, tops[0], tops[1])


def attn_far_kernel(
    d_ref, q_ref, k_ref, v_ref, hot_ref, hotq_ref, b_ref, acc_ref, top_ref, h0_ref, wout_ref, vec_ref,
    r1_ref, h1_ref, h1r_ref, ctx_s,
):
    rows = q_ref.shape[0]
    low = lane_low()
    mask = jnp.concatenate([place_mask(d_ref, rows, b, (1, rows), 1) for b in (2, 3)], axis=1)
    hot_own = hotq_ref[0:rows, :]
    for i in range(HEADS // 2):
        pair = slice(128 * i, 128 * (i + 1))
        outs = []
        for e in range(2):
            score, mine = pair_scores(
                e, q_ref[:, pair], k_ref[:, pair], hot_own, hot_ref, b_ref[2 * i + e], mask
            )
            old_top = top_ref[:, 128 * i + 64 * e : 128 * i + 64 * e + 1]
            top = jnp.maximum(jnp.max(score, axis=1, keepdims=True), old_top)
            weight = jnp.exp(score - top).astype(bf16)
            acc = dot_nn(weight, jnp.where(mine, v_ref[:, pair], bf16(1)))
            acc = acc + acc_ref[2 * i + e] * jnp.exp(old_top - top)
            outs.append(acc / pltpu.roll(acc, 64, 1))
        ctx_s[:, pair] = jnp.where(low, outs[0], outs[1]).astype(bf16)
    resid = h0_ref[...] + (dot_nn(ctx_s[...], wout_ref[...]) + vec_ref[0:1, :])
    r1_ref[...] = resid
    hidden = norm_parts(resid)[0] * vec_ref[1:2, :] + vec_ref[2:3, :]
    h1_ref[...] = hidden
    h1r_ref[...] = hidden.astype(bf16)


def attn_near(scalars, q, k, v, hot, bias):
    rows, width = q.shape
    return resident(
        attn_near_kernel, 5, (scalars, q, k, v, hot, bias),
        [((HEADS, rows, 128), f32), ((rows, width), f32)],
    )


def attn_far(scalars, q, k, v, hot, hot_near, bias, acc, top, h0, w_out, vec):
    rows, width = q.shape
    return resident(
        attn_far_kernel, 7,
        (scalars, q, k, v, hot, hot_near, bias, acc, top, h0, w_out, vec),
        [((rows, width), f32), ((rows, width), f32), ((rows, width), bf16)],
        [((rows, width), bf16)],
    )


def gelu_parts(u):
    phi = 0.5 + 0.5 * lax.erf(u * 0.7071067811865476)
    dens = jnp.exp(-0.5 * (u * u)) * 0.3989422804014327
    return u * phi, phi + u * dens


def norm_back(grad, xhat, rstd, gain):
    scaled = grad * gain
    mean_a = jnp.mean(scaled, axis=-1, keepdims=True)
    mean_b = jnp.mean(scaled * xhat, axis=-1, keepdims=True)
    return rstd * (scaled - mean_a - xhat * mean_b)


def col_sum(values):
    return jnp.sum(values, axis=0, keepdims=True)


def ffn_fwd_kernel(
    h1r_ref, wup_ref, bup_ref, wdown_ref, h1_ref, cot_ref, vec_ref,
    out_ref, dy_ref, dr2_ref, gp_ref, sums_ref,
):
    width = h1_ref.shape[1]
    h1r = h1r_ref[...]
    total = vec_ref[3:4, :]
    for c in range(0, wup_ref.shape[1], width):
        part = slice(c, c + width)
        g, slope = gelu_parts(dot_nn(h1r, wup_ref[:, part]) + bup_ref[0:1, part])
        gp_ref[:, part] = slope.astype(bf16)
        total = total + dot_nn(g.astype(bf16), wdown_ref[part, :])
    gain = vec_ref[4:5, :]
    xhat, rstd = norm_parts(h1_ref[...] + total)
    out_ref[0, 0] = (xhat * gain + vec_ref[5:6, :]).astype(bf16)
    grad = cot_ref[0, 0].astype(f32)
    dr2 = norm_back(grad, xhat, rstd, gain)
    dr2_ref[...] = dr2
    dy = dr2.astype(bf16)
    dy_ref[...] = dy
    sums_ref[0:1, :] = col_sum(dy.astype(f32))
    sums_ref[1:2, :] = col_sum(grad * xhat)
    sums_ref[2:3, :] = col_sum(grad)
    sums_ref[3:8, :] = jnp.zeros((5, width), f32)


def ffn_fwd(h1r, w_up, b_up, w_down, h1, cot, vec):
    rows, width = h1.shape
    return resident(
        ffn_fwd_kernel, 5, (h1r, w_up, b_up, w_down, h1, cot, vec),
        [
            (cot.shape, bf16), ((rows, width), bf16), ((rows, width), f32),
            ((rows, w_up.shape[1]), bf16), ((8, width), f32),
        ],
        scalars=0,
    )


def ffn_bwd_kernel(
    d_ref, dy_ref, wdown_ref, gp_ref, wup_ref, dr2_ref, r1_ref, vec_ref,
    dr1_ref, da_ref, sums_ref, upq_ref, downq_ref,
):
    width = dr2_ref.shape[1]
    size = upq_ref.shape[1]
    own = pl.ds(pl.multiple_of(d_ref[0] * size, 128), size)
    upq_ref[...] = wup_ref[:, own]
    downq_ref[...] = wdown_ref[own, :]
    dy = dy_ref[...]
    grad = dr2_ref[...]
    for c in range(0, wup_ref.shape[1], width):
        part = slice(c, c + width)
        du = (dot_nt(dy, wdown_ref[part, :]) * gp_ref[:, part].astype(f32)).astype(bf16)
        grad = grad + dot_nt(du, wup_ref[:, part])
    xhat, rstd = norm_parts(r1_ref[...])
    dr1 = norm_back(grad, xhat, rstd, vec_ref[1:2, :])
    dr1_ref[...] = dr1
    da = dr1.astype(bf16)
    da_ref[...] = da
    sums_ref[0:1, :] = col_sum(da.astype(f32))
    sums_ref[1:2, :] = col_sum(grad * xhat)
    sums_ref[2:3, :] = col_sum(grad)
    sums_ref[3:4, :] = col_sum(dr1)
    sums_ref[4:8, :] = jnp.zeros((4, width), f32)


def ffn_bwd(scalars, dy, w_down, gp, w_up, dr2, r1, vec):
    rows, width = dr2.shape
    size = w_up.shape[1] // 4
    return resident(
        ffn_bwd_kernel, 1, (scalars, dy, w_down, gp, w_up, dr2, r1, vec),
        [
            ((rows, width), f32), ((rows, width), bf16), ((8, width), f32),
            ((width, size), bf16), ((size, width), bf16),
        ],
    )


def ffn_again_kernel(d_ref, *refs):
    h1_refs, (wup_ref, bup_ref, g_ref, gp_ref) = refs[:4], refs[4:]
    rows = h1_refs[0].shape[0]
    part = g_ref.shape[1]
    w_up = wup_ref[...]
    b_up = bup_ref[0:1, pl.ds(pl.multiple_of(d_ref[0] * part, 128), part)]
    for b in range(4):
        g, slope = gelu_parts(dot_nn(h1_refs[b][...], w_up) + b_up)
        g_ref[b * rows : (b + 1) * rows, :] = g.astype(bf16)
        gp_ref[b * rows : (b + 1) * rows, :] = slope.astype(bf16)


def ffn_again(scalars, h1_blocks, up_own, b_up):
    rows = h1_blocks[0].shape[0]
    part = up_own.shape[1]
    return resident(
        ffn_again_kernel, 2, (scalars, *h1_blocks, up_own, b_up), [((4 * rows, part), bf16)] * 2
    )


def bit_of(d_ref, bit):
    return (d_ref[3] >> bit) & 1


def store_shares(bit, pieces, send_ref, keep_ref):
    half = len(pieces) // 2
    for mine in (0, 1):

        @pl.when(bit == mine)
        def _():
            for n, piece in enumerate(pieces):
                ref = keep_ref if n // half == mine else send_ref
                ref[n % half] = piece()


def owner_order(pages, bits):
    count = len(bits)
    return [sum(((n >> (count - 1 - k)) & 1) << bit for k, bit in enumerate(bits)) for n in range(pages)]


def down_kernel(bit, order, d_ref, g_ref, *refs):
    ctx_refs, dy_refs, da_refs, (send_ref, keep_ref, dy_s, da_s, res_s) = refs[:3], refs[3:7], refs[7:11], refs[11:]
    rows, width = dy_refs[0].shape
    for b in range(4):
        dy_s[b * rows : (b + 1) * rows, :] = dy_refs[b][...]
        da_s[b * rows : (b + 1) * rows, :] = da_refs[b][...]
    size = g_ref.shape[1]
    for n in range(0, size, 256):
        res_s[n : n + 256, :] = dot_tn(g_ref[:, n : n + 256], dy_s[...]).astype(bf16)
    ctx = jnp.concatenate([ref[...] for ref in ctx_refs], axis=0)
    res_s[size:, :] = dot_nn(ctx, da_s[...]).astype(bf16)
    pages = len(order)
    down, out = size // pages, ctx.shape[0] // pages

    def piece(owner):
        return lambda: jnp.concatenate(
            [
                res_s[owner * down : (owner + 1) * down, :].astype(f32),
                res_s[size + owner * out : size + (owner + 1) * out, :].astype(f32),
            ],
            axis=0,
        ).astype(bf16)

    store_shares(bit_of(d_ref, bit), [piece(owner) for owner in order], send_ref, keep_ref)


def down_grad(scalars, bit, order, g_q, ctxs, dy_blocks, da_blocks):
    rows, width = dy_blocks[0].shape
    size, out = g_q.shape[1], len(ctxs) * ctxs[0].shape[0]
    pages = len(order)
    share = ((pages // 2, (size + out) // pages, width), bf16)
    return resident(
        functools.partial(down_kernel, bit, order), 0.02, (scalars, g_q, *ctxs, *dy_blocks, *da_blocks),
        [share, share],
        [((4 * rows, width), bf16), ((4 * rows, width), bf16), ((size + out, width), bf16)],
    )


def up_kernel(bit, order, d_ref, gp_ref, wdown_ref, *refs):
    dy_refs, h1_refs, (send_ref, keep_ref, sums_ref, du_s, h1_s, res_s) = refs[:4], refs[4:8], refs[8:]
    rows, width = dy_refs[0].shape
    w_down = wdown_ref[...]
    for b in range(4):
        part = slice(b * rows, (b + 1) * rows)
        du = (dot_nt(dy_refs[b][...], w_down) * gp_ref[part, :].astype(f32)).astype(bf16)
        du_s[part, :] = du
        h1_s[part, :] = h1_refs[b][...]
        total = col_sum(du.astype(f32))
        sums = total if b == 0 else sums + total
    sums_ref[...] = jnp.broadcast_to(sums, sums_ref.shape)
    for n in range(0, width, 256):
        res_s[n : n + 256, :] = dot_tn(h1_s[:, n : n + 256], du_s[...])
    pages = len(order)
    own = width // 4
    rows = own // pages

    def piece(owner):
        starts = [q * own + owner * rows for q in (0, 2, 1, 3)]
        return lambda: jnp.stack([res_s[n : n + rows, :].astype(bf16) for n in starts])

    store_shares(bit_of(d_ref, bit), [piece(owner) for owner in order], send_ref, keep_ref)


def up_grad(scalars, bit, order, gp_q, down_own, dy_blocks, h1_blocks):
    rows, width = dy_blocks[0].shape
    part = gp_q.shape[1]
    pages = len(order)
    share = ((pages // 2, 4, width // 4 // pages, part), bf16)
    return resident(
        functools.partial(up_kernel, bit, order), 2,
        (scalars, gp_q, down_own, *dy_blocks, *h1_blocks),
        [share, share, ((8, part), f32)],
        [((4 * rows, part), bf16), ((4 * rows, width), bf16), ((width, part), f32)],
    )


def step_kernel(bit, d_ref, keep_ref, got_ref, *out_refs):
    half = keep_ref.shape[0] // 2
    mine = bit_of(d_ref, bit)
    for ref, at in zip(out_refs, (1 - mine, mine)):
        part = pl.ds(at * half, half)
        ref[...] = (keep_ref[part].astype(f32) + got_ref[part].astype(f32)).astype(bf16)


def step_sum(scalars, bit, keep, got):
    half = (keep.shape[0] // 2,) + keep.shape[1:]
    kernel = functools.partial(step_kernel, bit)
    return resident(kernel, 0.02, (scalars, keep, got), [(half, bf16)] * 2)


def last_kernel(keep_ref, got_ref, out_ref):
    out_ref[...] = (keep_ref[0].astype(f32) + got_ref[0].astype(f32)).astype(bf16)


def last_sum(keep, got):
    return resident(last_kernel, 0.02, (keep, got), [(keep.shape[1:], bf16)], scalars=0)[0]


def last_turn_kernel(d_ref, keep_ref, got_ref, send_ref, stay_ref):
    for ref, seq in ((send_ref, 1 - d_ref[5]), (stay_ref, d_ref[5])):
        part = pl.ds(2 * seq, 2)
        ref[...] = (keep_ref[0, part].astype(f32) + got_ref[0, part].astype(f32)).astype(bf16)


def last_turn(scalars, keep, got):
    shape = (2,) + keep.shape[2:]
    return resident(last_turn_kernel, 0.02, (scalars, keep, got), [(shape, bf16)] * 2)


def far_turn_kernel(d_ref, keep_ref, got_ref, send_ref, stay_ref):
    for ref, stream in ((send_ref, 1 - d_ref[4]), (stay_ref, d_ref[4])):
        ref[0] = keep_ref[stream]
        ref[1] = got_ref[stream]


def far_turn(scalars, keep, got):
    shape = (2,) + keep.shape[1:]
    return resident(far_turn_kernel, 0.02, (scalars, keep, got), [(shape, bf16)] * 2)


def join_kernel(one_ref, two_ref, out_ref):
    half = one_ref.shape[0]
    out_ref[0:half] = one_ref[...]
    out_ref[half:] = two_ref[...]


def join(one, two):
    shape = (2 * one.shape[0],) + one.shape[1:]
    return resident(join_kernel, 0.02, (one, two), [(shape, bf16)], scalars=0)[0]


def weights_kernel(
    head, d_ref, h0a_ref, h0b_ref, warr_ref, barr_ref, hota_ref, hotb_ref, b_ref,
    p_ref, kat_ref, et_ref, r_ref, ctx_ref,
):
    rows = h0a_ref.shape[0] // 2
    half = 2 * rows
    low = lane_low()
    one = jnp.ones((), bf16)
    mask = jnp.concatenate([place_mask(d_ref, rows, b, (1, rows), 1) for b in range(4)], axis=1)
    hots = (hota_ref, hotb_ref)
    cols = slice(256 * head, 256 * (head + 1))
    for n, ref in enumerate((h0a_ref, h0b_ref)):
        part = slice(half * n, half * (n + 1))
        p_ref[part, :] = (dot_nn(ref[...], warr_ref[:, cols]) + barr_ref[0:1, cols]).astype(bf16)
    kv = p_ref[:, 0:128]
    hot = jnp.concatenate([hota_ref[...], hotb_ref[...]], axis=0)
    k_aug = jnp.concatenate([jnp.where(low, kv, hot[:, 0:128]), hot[:, 128:256]], axis=1)
    kat_ref[...] = k_aug.T
    v_one_t = jnp.where(low, one, kv).T
    bias = b_ref[d_ref[0] * (HEADS // 4) + head]
    for block in range(4):
        part = slice(rows * block, rows * (block + 1))
        hot_q = hots[block // 2][rows * (block % 2) : rows * (block % 2 + 1), :]
        q_only = p_ref[part, 128:256] * bf16(0.125)
        side = dot_nn(hot_q, bias).astype(bf16)
        q_aug = jnp.concatenate([jnp.where(low, q_only, side[:, 0:128]), side[:, 128:256]], axis=1)
        score = dot_nt(q_aug, k_aug) + mask
        top = jnp.max(score, axis=1, keepdims=True)
        weight = jnp.exp(score - top).astype(bf16)
        et_ref[:, part] = weight.T
        acc = dot_nt(v_one_t, weight)
        recip = 1.0 / acc[0:8, :]
        r_ref[:, part] = recip
        ctx_ref[:, part] = (acc[64:128, :] * recip[0:1, :]).astype(bf16)


def own_weights(head, scalars, h0_near, h0_far, w_arr, b_arr, hot_near, hot_far, bias):
    keys = 2 * h0_near.shape[0]
    return resident(
        functools.partial(weights_kernel, head), 1,
        (scalars, h0_near, h0_far, w_arr, b_arr, hot_near, hot_far, bias),
        [
            ((keys, 256), bf16), ((256, keys), bf16), ((keys, keys), bf16), ((8, keys), f32),
            ((64, keys), bf16),
        ],
    )


def turned_kernel(near_ref, far_ref, out_ref):
    half = near_ref.shape[0]
    out_ref[:, 0:half] = near_ref[...].T
    out_ref[:, half:] = far_ref[...].T


def turned(near, far):
    return resident(
        turned_kernel, 0.5, (near, far), [((near.shape[1], 2 * near.shape[0]), bf16)], scalars=0
    )[0]


def attn_bwd_kernel(head, h0t_ref, *refs):
    da_refs = refs[:4]
    p_ref, kat_ref, et_ref, r_ref, warr_ref, oarr_ref, hota_ref, hotb_ref = refs[4:12]
    dp_ref, dw_ref, tab_ref, row_ref = refs[12:]
    rows, width = da_refs[0].shape
    keys = 4 * rows
    low = lane_low()
    zero = jnp.zeros((), bf16)
    cols = slice(256 * head, 256 * (head + 1))
    v_only = jnp.where(low, zero, p_ref[:, 0:128])
    k_aug_t = kat_ref[...]
    oarr = oarr_ref[128 * head : 128 * (head + 1), :]
    w_arr = warr_ref[:, cols]
    hots = (hota_ref, hotb_ref)
    acc_kv = jnp.zeros((keys, 128), f32)
    acc_b = jnp.zeros((256, 256), f32)
    for block in range(4):
        part = slice(rows * block, rows * (block + 1))
        q_only = p_ref[part, 128:256] * bf16(0.125)
        hot_q = hots[block // 2][rows * (block % 2) : rows * (block % 2 + 1), :]
        recip = r_ref[:, part]
        dc = (dot_nt(da_refs[block][...], oarr) * recip.T[:, 0:1]).astype(bf16)
        weight_low = et_ref[:, part]
        weight = weight_low.astype(f32)
        dweight = dot_nt(v_only, dc)
        inner = jnp.sum(weight * dweight, axis=0, keepdims=True) * recip[0:1, :]
        dscore = (weight * (dweight - inner)).astype(bf16)
        acc_kv = acc_kv + (dot_nn(dscore, q_only) + dot_nn(weight_low, dc))
        dq_aug_t = dot_nn(k_aug_t, dscore)
        dq = dq_aug_t[0:128, :].T * 0.125
        dp_ref[part, 128:256] = jnp.where(low, dq, 0.0).astype(bf16)
        acc_b = acc_b + dot_nn(dq_aug_t.astype(bf16), hot_q)
    dp_ref[:, 0:128] = acc_kv.astype(bf16)
    dp = dp_ref[...]
    dw_ref[...] = dot_nn(h0t_ref[...], dp)
    total = col_sum(dp.astype(f32))
    row_ref[...] = jnp.zeros(row_ref.shape, f32)
    row_ref[0:1, 0:256] = total
    high = total.astype(bf16)
    rest = (total - high.astype(f32)).astype(bf16)
    lang = dot_nt(jnp.broadcast_to(high, (8, 256)), w_arr)
    lang = lang + dot_nt(jnp.broadcast_to(rest, (8, 256)), w_arr)
    row_ref[1:2, :] = lang[0:1, :]
    for first, block in (
        (0, acc_b[64:96, 0:128]), (32, acc_b[96:128, 0:128]), (64, acc_b[128:256, 128:256]),
    ):
        size = block.shape[0]
        lane = iota((size, 128), 1)
        key = iota((size, 128), 0)
        if first == 32:
            lane = lane - 32
        index = jnp.clip(key - lane, -16, 15) + 16
        if size == 32:
            index = jnp.where(jnp.logical_and(lane >= 0, lane < 32), index, -1)
        for bucket in range(32):
            at = first + bucket
            tab_ref[at : at + 1, :] = col_sum(jnp.where(index == bucket, block, 0.0))


def attn_bwd(head, h0_t, da_blocks, p_all, kat, et, recip, w_arr, o_arr, hot_near, hot_far):
    rows, width = da_blocks[0].shape
    keys = 4 * rows
    return resident(
        functools.partial(attn_bwd_kernel, head), 0.02,
        (h0_t, *da_blocks, p_all, kat, et, recip, w_arr, o_arr, hot_near, hot_far),
        [((keys, 256), bf16), ((width, 256), f32), ((96, 128), f32), ((8, width), f32)],
        scalars=0,
    )


def input_kernel(*refs):
    dp_refs, (warr_ref, dr1_ref, own_ref, near_ref, far_ref) = refs[:3], refs[3:]
    rows = dr1_ref.shape[0]
    dp = jnp.concatenate([ref[...] for ref in dp_refs], axis=1)
    for b in (1, 3, 2, 0):
        part = dot_nt(dp[b * rows : (b + 1) * rows, :], warr_ref[...])
        if b == 0:
            own_ref[...] = dr1_ref[...] + part
        elif b == 2:
            far_ref[...] = part
        else:
            near_ref[(b // 2) * rows : (b // 2 + 1) * rows, :] = part.astype(bf16)


def input_parts(dps, w_arr, dr1):
    rows, width = dr1.shape
    return resident(
        input_kernel, 0.02, (*dps, w_arr, dr1),
        [((rows, width), f32), ((2 * rows, width), bf16), ((rows, width), f32)], scalars=0,
    )


def far_kernel(part_ref, got_ref, out_ref):
    rows = part_ref.shape[0]
    out_ref[...] = (part_ref[...] + got_ref[rows:, :].astype(f32)).astype(bf16)


def far_share(far_part, got_near):
    return resident(far_kernel, 0.02, (far_part, got_near), [(far_part.shape, bf16)], scalars=0)[0]


def input_sum_kernel(own_ref, near_ref, far_ref, out_ref):
    rows = own_ref.shape[0]
    total = own_ref[...] + near_ref[0:rows, :].astype(f32) + far_ref[...].astype(f32)
    out_ref[0, 0] = total.astype(bf16)


def input_sum(own_part, got_near, got_far):
    shape = (1, 1) + own_part.shape
    return resident(
        input_sum_kernel, 0.02, (own_part, got_near, got_far), [(shape, bf16)], scalars=0
    )[0]


SMALL_ROWS = 96


def pack_kernel(bit, order, d_ref, *refs):
    one_ref, two_ref, up_ref = refs[:3]
    dw_refs, row_refs, tab_refs, (send_ref, keep_ref, m_s) = refs[3:6], refs[6:9], refs[9:12], refs[12:]
    quarter, language = d_ref[0], d_ref[2]
    pages = len(order)
    own = HEADS // 4
    cols = own * 64
    n = cols // pages
    m_s[...] = jnp.zeros(m_s.shape, f32)
    lang = one_ref[3:4, :]
    for ref in row_refs:
        lang = lang + ref[1:2, :]
    vectors = [one_ref[k : k + 1, :] for k in range(3)] + [two_ref[k : k + 1, :] for k in range(3)]
    vectors += [None, None, None, None, None, None]
    vectors += [jnp.where(language == k, lang, 0.0) for k in range(7)]
    lane = iota((32, 128), 1)
    tables = [jnp.zeros((32, 128), f32) for _ in range(3)]
    for j in range(own):
        sums = jnp.sum(tab_refs[j][...], axis=1, keepdims=True)
        for t in range(3):
            at = 12 * t + quarter * own + j
            tables[t] = jnp.where(lane == at, sums[32 * t : 32 * (t + 1), :], tables[t])
    table = tables[0] + tables[1] + tables[2]
    for q in range(4):
        mine = quarter == q
        for k, vector in enumerate(vectors):
            if vector is not None:
                for part in range(own):
                    first = q * cols + 64 * part
                    m_s[q, 3 * k + part : 3 * k + part + 1, 0:64] = vector[:, first : first + 64]
        for j in range(own):
            row = row_refs[j]
            m_s[q, 18 + j : 19 + j, 0:64] = jnp.where(mine, row[0:1, 128:192], 0.0)
            m_s[q, 21 + j : 22 + j, 0:64] = jnp.where(mine, row[0:1, 64:128], 0.0)
        for k in range(12):
            m_s[q, 24 + k : 25 + k, 0:64] = jnp.where(mine, up_ref[0:1, 64 * k : 64 * (k + 1)], 0.0)
        m_s[q, 64:72, 0:64] = table[8 * q : 8 * (q + 1), 0:64]
    share = SMALL_ROWS // pages
    zeros = jnp.zeros((n - share, 64), f32)

    def block(p, q):
        first = q * cols + p * n
        pieces = [ref[first : first + n, 64 * t : 64 * (t + 1)] for t in range(3) for ref in dw_refs]
        small = m_s[q, p * share : (p + 1) * share, 0:64]
        pieces.append(jnp.concatenate([small, zeros], axis=0))
        return jnp.concatenate(pieces, axis=1).astype(bf16)

    def piece(p):
        return lambda: jnp.stack([block(p, q) for q in (0, 2, 1, 3)])

    store_shares(bit_of(d_ref, bit), [piece(p) for p in order], send_ref, keep_ref)


def pack(scalars, bit, order, sums_one, sums_two, sums_up, dws, rows_out, tabs):
    pages = len(order)
    n = dws[0].shape[0] // 4 // pages
    return resident(
        functools.partial(pack_kernel, bit, order), 0.02,
        (scalars, sums_one, sums_two, sums_up, *dws, *rows_out, *tabs),
        [((pages // 2, 4, n, 640), bf16)] * 2, [((4, SMALL_ROWS, 128), f32)],
    )


def heads_kernel(distances, d_ref, *refs):
    got_refs, (key_ref, value_ref, query_ref, small_s) = parts_of(refs[:-4]), refs[-4:]
    pages = len(got_refs)
    share = SMALL_ROWS // pages
    for ref, distance in zip(got_refs, distances):
        page = d_ref[3] ^ distance
        blocks = [ref[d_ref[0] ^ q].astype(f32) for q in range(4)]
        for t, out_ref in enumerate((key_ref, value_ref, query_ref)):
            out_ref[page] = jnp.concatenate(
                [block[:, 192 * t : 192 * (t + 1)] for block in blocks], axis=1
            )
        total = (blocks[0] + blocks[1]) + (blocks[2] + blocks[3])
        small_s[page, :, 0:64] = total[0:share, 576:640]


def small_kernel(m_ref, vec_ref, lang_ref, tab_ref, m_s):
    pages, share, _ = m_ref.shape
    for p in range(pages):
        m_s[p * share : (p + 1) * share, :] = m_ref[p]
    vec_ref[...] = jnp.zeros(vec_ref.shape, f32)
    for k in range(8):
        for part in range(3):
            vec_ref[k : k + 1, 64 * part : 64 * (part + 1)] = m_s[3 * k + part : 3 * k + part + 1, 0:64]
    for k in range(12):
        vec_ref[8:9, 64 * k : 64 * (k + 1)] = m_s[24 + k : 25 + k, 0:64]
    for part in range(3):
        piece = jnp.concatenate(
            [m_s[36 + 3 * k + part : 37 + 3 * k + part, 0:64] for k in range(7)] + [jnp.zeros((1, 64), f32)], axis=0
        )
        lang_ref[64 * part : 64 * (part + 1), :] = piece.T[:, 0:7]
    for t in range(3):
        tab_ref[t] = m_s[64:72, 12 * t : 12 * (t + 1)]


def finish_heads(scalars, pieces, distances):
    _, _, n, _ = pieces[0].shape
    pages = len(distances)
    rows = pages * n
    mat = ((pages, n, 4 * rows), f32)
    *mats, small = resident(
        functools.partial(heads_kernel, distances), 0.2, (scalars, *pieces),
        [mat, mat, mat, ((pages, SMALL_ROWS // pages, 128), f32)],
    )
    vecs = resident(
        small_kernel, 0.2, (small,),
        [((16, 768), f32), ((rows, 7), f32), ((3, 8, HEADS), f32)],
        [((SMALL_ROWS, 128), f32)], scalars=0,
    )
    return [m.reshape(rows, 4 * rows) for m in mats] + list(vecs)


def parts_of(refs):
    return [ref.at[k] for ref in refs for k in range(ref.shape[0])]


def up_finish_kernel(distances, d_ref, *refs):
    out_ref = refs[-1]
    part = refs[0].shape[-1]
    for ref, distance in zip(parts_of(refs[:-1]), distances):
        for q in range(4):
            cols = pl.ds(pl.multiple_of((d_ref[0] ^ q) * part, 128), part)
            out_ref[d_ref[3] ^ distance, :, cols] = ref[q].astype(f32)


def finish_up(scalars, pieces, distances):
    _, _, n, part = pieces[0].shape
    pages = len(distances)
    kernel = functools.partial(up_finish_kernel, distances)
    rows = resident(kernel, 0.2, (scalars, *pieces), [((pages, n, 4 * part), f32)])[0]
    return rows.reshape(pages * n, 4 * part)


def down_finish_kernel(distances, d_ref, *refs):
    down_ref, out_ref = refs[-2:]
    down = down_ref.shape[1]
    for ref, distance in zip(parts_of(refs[:-2]), distances):
        owner = d_ref[3] ^ distance
        block = ref[...].astype(f32)
        down_ref[owner] = block[0:down, :]
        out_ref[owner] = block[down:, :]


def finish_down(scalars, pieces, size, out, distances):
    width = pieces[0].shape[2]
    pages = len(distances)
    blocks = resident(
        functools.partial(down_finish_kernel, distances), 0.2, (scalars, *pieces),
        [((pages, size // pages, width), f32), ((pages, out // pages, width), f32)],
    )
    return blocks[0].reshape(size, width), blocks[1].reshape(out, width)


def swap(values, axis, bit=0):
    size = lax.axis_size(axis)
    return lax.ppermute(values, axis, [(i, i ^ (1 << bit)) for i in range(size)])


def page_gather(own):
    near = swap(own, "seq")
    far = swap(own, "stream")
    return [own, near, far, swap(far, "seq")]


def page_xor(values, mask):
    pages = lax.axis_size("page")
    return lax.ppermute(values, "page", [(p, p ^ mask) for p in range(pages)])


def on_device(
    tokens, boxes, text_lengths, language, lang_table, w_query, b_query, w_key, w_value, b_value,
    w_out, b_out, norm1_gain, norm1_bias, w_up, b_up, w_down, b_down, norm2_gain, norm2_bias,
    table_pos, table_x, table_y, cotangent,
):
    rows = tokens.shape[2]
    width = tokens.shape[3]
    head_dim = width // HEADS
    own_heads = HEADS // 4
    own_cols = own_heads * head_dim
    pages = lax.axis_size("page")
    place = [lax.axis_index(axis).astype(i32).reshape(1) for axis in (("stream", "seq"), *PAGE_AXES)]
    scalars = jnp.concatenate([place[0], text_lengths, language, *place[1:]])

    h0, message = prep(language, tokens, boxes.reshape(2, 1, 1, rows), lang_table.T)
    near_msg, far_msg = swap(message, "seq"), swap(message, "stream")

    vec = jnp.concatenate(
        [b_out, norm1_gain, norm1_bias, b_down, norm2_gain, norm2_bias, b_query, b_value]
    )
    vec = vec.reshape(8, width).astype(f32)
    b_up_row = b_up[None, :].astype(f32)
    scalars = after(scalars, vec, b_up_row)
    bias = bias_mats(table_x.T, table_y.T, table_pos.T)

    k_near, v_near, hot_near, h0_near, q_own = project(
        scalars, message, near_msg, w_key, w_value, vec, 0, w_query
    )
    acc, top = attn_near(scalars, q_own, k_near, v_near, hot_near, bias)
    far_msg = after(far_msg, acc)
    last_msg = swap(far_msg, "seq")
    w_arr, b_arr, o_arr = pick_weights(after(scalars, acc), w_key, w_value, w_query, vec, w_out)
    last_msg = after(last_msg, w_arr)
    k_far, v_far, hot_far, h0_far = project(scalars, far_msg, last_msg, w_key, w_value, vec, 2)
    r1, h1, h1r = attn_far(
        scalars, q_own, k_far, v_far, hot_far, hot_near, bias, acc, top, h0, w_out, vec
    )
    h1_near, h1_far = swap(h1r, "seq"), swap(h1r, "stream")
    layer_out, dy, dr2, gp, sums_two = ffn_fwd(h1r, w_up, b_up_row, w_down, h1, cotangent, vec)
    dy_near, dy_far = swap(dy, "seq"), swap(dy, "stream")
    dr1, da, sums_one, up_own, down_own = ffn_bwd(scalars, dy, w_down, gp, w_up, dr2, r1, vec)
    da_near, da_far = swap(da, "seq"), swap(da, "stream")

    def weights(j, order_on):
        return own_weights(
            j, after(scalars, order_on), h0_near, h0_far, w_arr, b_arr, hot_near, hot_far, bias
        )

    own = [weights(0, (da, h1_far))]
    h1_blocks = [h1r, h1_near, h1_far, swap(h1_far, "seq")]
    own.append(weights(1, own[0][0]))
    own.append(weights(2, own[1][0]))
    dy_far = after(dy_far, own[2][0])
    dy_blocks = [dy, dy_near, dy_far, swap(dy_far, "seq")]
    g_q, gp_q = ffn_again(after(scalars, own[2][0]), h1_blocks, up_own, b_up_row)

    bits = list(range(pages.bit_length() - 1))
    order = owner_order(pages, bits)
    up_send, up_keep, sums_up = up_grad(
        scalars, bits[0], order, gp_q, down_own, dy_blocks, h1_blocks
    )
    up_got = page_xor(up_send, 1)
    h0_t = turned(after(h0_near, up_keep), h0_far)
    da_far = after(da_far, h0_t)
    da_blocks = [da, da_near, da_far, swap(da_far, "seq")]
    down_send, down_keep = down_grad(
        scalars, bits[0], order, g_q, [o[4] for o in own], dy_blocks, da_blocks
    )
    down_got = page_xor(down_send, 1)

    state = {"up": (up_keep, up_got, 1), "down": (down_keep, down_got, 1)}

    def advance(name, order_on):
        keep, got, at = state[name]
        send, keep = step_sum(scalars, bits[at], *after((keep, got), order_on))
        state[name] = (keep, page_xor(send, 1 << bits[at]), at + 1)
        return keep

    def turn_one(name, order_on):
        keep, got, _ = state[name]
        send, keep = last_turn(scalars, *after((keep, got), order_on))
        state[name] = (keep, swap(send, "seq"))
        return keep

    def turn_two(name, order_on):
        send, keep = far_turn(scalars, *after(state[name], order_on))
        state[name] = (keep, swap(send, "stream"))
        return keep

    def begin(name, mine, path):
        state[name] = (mine, page_xor(mine, 1 << path[0]), path[1:], [0, 1 << path[0]])
        return mine

    def widen(name, order_on):
        mine, got, path, masks = state[name]
        mine = join(*after((mine, got), order_on))
        state[name] = (mine, page_xor(mine, 1 << path[0]), path[1:], masks + [m | 1 << path[0] for m in masks])
        return mine

    def backward(j, order_on):
        p_own, kat, et, recip, _ = own[j]
        return attn_bwd(
            j, h0_t, da_blocks, p_own, after(kat, order_on), et, recip, w_arr, o_arr, hot_near, hot_far
        )

    heads = [backward(0, down_keep)]
    heads.append(backward(1, heads[0][0]))
    last = advance("up", heads[1][0])
    heads.append(backward(2, last))
    dps, dws, tabs, rows_out = zip(*heads)
    heads_send, heads_keep = pack(
        scalars, bits[0], order, sums_one, sums_two, sums_up, dws, rows_out, tabs
    )
    state["head"] = (heads_keep, page_xor(heads_send, 1), 1)
    last = advance("up", heads_keep)
    last = advance("down", last)
    own_part, near_part, far_part = input_parts(dps, after(w_arr, last), dr1)
    got_near = swap(near_part, "seq")
    last = advance("head", own_part)
    for _ in bits[3:]:
        last = advance("up", last)
        last = advance("down", last)
    last = turn_one("up", last)
    last = advance("down", last)
    last = turn_two("up", last)
    far_sum = far_share(far_part, after(got_near, last))
    got_far = swap(far_sum, "stream")
    last = advance("head", far_sum)
    for _ in bits[3:]:
        last = advance("head", last)
    back = bits[::-1]
    last = begin("up", join(*after(state["up"], last))[None], bits[:1] + back[:-1])
    keep, got, _ = state["down"]
    last = begin("down", last_sum(*after((keep, got), last))[None], back)
    last = widen("up", last)
    last = turn_one("head", last)
    last = turn_two("head", last)
    last = widen("down", last)
    last = begin("head", join(*after(state["head"], last))[None], back)
    for _ in bits[2:]:
        last = widen("up", last)
    input_grad = input_sum(after(own_part, last), got_near, got_far)
    last = widen("head", input_grad)
    for _ in bits[2:]:
        last = widen("down", last)
        last = widen("head", last)
    mine, got, _, masks = state["up"]
    res_up = finish_up(after(scalars, last), [mine, got], masks)
    mine, got, _, masks = state["down"]
    res_down, res_out = finish_down(
        after(scalars, res_up), [mine, got], w_up.shape[1] // 4, own_cols, masks
    )
    mine, got, _, masks = state["head"]
    res_key, res_value, res_query, vecs, s_lang, s_tab = finish_heads(
        after(scalars, res_down), [mine, got], masks
    )
    s_bout, s_g1, s_s1, s_bdown, s_g2, s_s2, s_bq, s_bv = (vecs[i, :own_cols] for i in range(8))
    return (
        layer_out, input_grad, s_lang, res_query, s_bq, res_key, res_value, s_bv,
        res_out, s_bout, s_g1, s_s1, res_up, vecs[8], res_down, s_bdown, s_g2, s_s2,
        s_tab[2], s_tab[0], s_tab[1],
    )


def solution(mesh):
    token_spec = P("page", "stream", "seq", None)
    rep = P()
    in_specs = (
        (token_spec, P(None, "page", "stream", "seq"), P("page"), P("page"))
        + (rep,) * 19
        + (token_spec,)
    )
    mat, vec = P(("stream", "seq"), None), P(("stream", "seq"))
    out_specs = (
        token_spec, token_spec, mat, mat, vec, mat, mat, vec, mat, vec, vec, vec,
        mat, vec, mat, vec, vec, vec, mat, mat, mat,
    )
    return jax.shard_map(
        on_device, mesh=mesh, in_specs=in_specs, out_specs=out_specs, check_vma=False
    )
```

```python
import functools

import jax
import jax.numpy as jnp
import numpy as np
from jax import lax
from jax.experimental import pallas as pl
from jax.experimental.pallas import tpu as pltpu
from jax.sharding import PartitionSpec as P

HEADS = 12
BOX_ROWS = 16
norm_eps = 1e-05
masked_score = -1000000000.0
level_step = 8
f32 = jnp.float32
bf16 = jnp.bfloat16
i32 = jnp.int32
MB = 1 << 20
SCOPED_MB = 12
PAGE_AXES = ("page", "stream", "seq")


def dot_nn(left, right):
    return lax.dot_general(left, right, (((1,), (0,)), ((), ())), preferred_element_type=f32)


def dot_nt(left, right):
    return lax.dot_general(left, right, (((1,), (1,)), ((), ())), preferred_element_type=f32)


def dot_tn(left, right):
    return lax.dot_general(left, right, (((0,), (0,)), ((), ())), preferred_element_type=f32)


def params(vmem_mb):
    return pltpu.CompilerParams(
        vmem_limit_bytes=vmem_mb * MB, dimension_semantics=("arbitrary",)
    )


def struct(shape, kind):
    return jax.ShapeDtypeStruct(shape, kind)


def whole(shape):
    return pl.BlockSpec(shape, lambda *at: (0,) * len(shape))


def fixed(shape, at):
    return pl.BlockSpec(shape, lambda *_: at)


def iota(shape, dim):
    return lax.broadcasted_iota(i32, shape, dim)


def lane_low():
    return iota((1, 128), 1) < 64


SMEM = pl.BlockSpec(memory_space=pltpu.SMEM)
VMEM = pl.BlockSpec(memory_space=pltpu.VMEM)
HBM = pl.BlockSpec(memory_space=pltpu.HBM)


def cost(micros):
    return pl.CostEstimate(
        flops=int(micros * 1.15e10), bytes_accessed=int(micros * 3.69e7), transcendentals=0
    )


def resident(kernel, micros, args, outs, scratch=(), scalars=1):
    return pl.pallas_call(
        kernel,
        cost_estimate=cost(micros),
        in_specs=[SMEM] * scalars + [VMEM] * (len(args) - scalars),
        out_specs=[VMEM] * len(outs),
        out_shape=[struct(*out) for out in outs],
        scratch_shapes=[pltpu.VMEM(*entry) for entry in scratch],
        compiler_params=pltpu.CompilerParams(vmem_limit_bytes=SCOPED_MB * MB),
    )(*args)


def after(values, *others):
    return lax.optimization_barrier((values, others))[0]


def fetch(refs, buffers, sems):
    copies = [
        pltpu.make_async_copy(ref, buffer, sems.at[k])
        for k, (ref, buffer) in enumerate(zip(refs, buffers))
    ]
    for copy in copies:
        copy.start()
    for copy in copies:
        copy.wait()


def prep_kernel(
    lang_ref, len_ref, tok_ref, box_ref, table_ref, info_ref, h0_ref, msg_ref, tok_s, box_s, table_s, sems
):
    stream, seq = lax.axis_index("stream"), lax.axis_index("seq")
    values = (2 * stream + seq, len_ref[0], lang_ref[0], lax.axis_index("page"), stream, seq)
    for k, value in enumerate(values):
        info_ref[k] = value
    fetch((tok_ref, box_ref, table_ref), (tok_s, box_s, table_s), sems)
    rows, width = h0_ref.shape
    pick = (iota((8, table_s.shape[0]), 1) == lang_ref[0]).astype(bf16)
    column = dot_nn(pick, table_s[...])[0:1, :]
    h0 = tok_s[0, 0].astype(f32) + column
    h0_ref[...] = h0
    msg_ref[0:rows, :] = h0.astype(bf16)
    row = iota((BOX_ROWS, rows), 0)
    box_x = jnp.broadcast_to(box_s[0, 0], (BOX_ROWS, rows)).astype(f32)
    box_y = jnp.broadcast_to(box_s[1, 0], (BOX_ROWS, rows)).astype(f32)
    packed = jnp.where(row == 0, box_x, jnp.where(row == 1, box_y, 0.0)).astype(bf16)
    msg_ref[rows : rows + BOX_ROWS, :] = jnp.zeros((BOX_ROWS, width), bf16)
    msg_ref[rows : rows + BOX_ROWS, 0:rows] = packed


def fetching(kernel, micros, scalars, arrays, outs):
    return pl.pallas_call(
        kernel,
        cost_estimate=cost(micros),
        in_specs=[SMEM] * len(scalars) + [HBM] * len(arrays),
        out_specs=[SMEM if out[1] == i32 else VMEM for out in outs],
        out_shape=[struct(*out) for out in outs],
        scratch_shapes=[pltpu.VMEM(a.shape, a.dtype) for a in arrays]
        + [pltpu.SemaphoreType.DMA((len(arrays),))],
        compiler_params=pltpu.CompilerParams(vmem_limit_bytes=SCOPED_MB * MB),
    )(*scalars, *arrays)


def prep(language, text_lengths, tokens, boxes, lang_table):
    rows, width = tokens.shape[2:]
    return fetching(
        prep_kernel, 1, (language, text_lengths), (tokens, boxes, lang_table),
        [((6,), i32), ((rows, width), f32), ((rows + BOX_ROWS, width), bf16)],
    )


def consts_kernel(*refs):
    count = (len(refs) - 4) // 2
    (out_ref, vec_ref, up_ref), scratch, sems = refs[count : count + 3], refs[count + 3 : -1], refs[-1]
    fetch(refs[:count], scratch, sems)
    vectors, up_s, tables = scratch[:8], scratch[8], scratch[9:]
    for k, vector in enumerate(vectors):
        vec_ref[k : k + 1, :] = vector[...].astype(f32).reshape(1, vec_ref.shape[1])
    up_ref[...] = up_s[...].astype(f32).reshape(up_ref.shape)
    bucket = jnp.clip(iota((32, 256), 1) - 128, -16, 15) + 16
    marks = (bucket == iota((32, 256), 0)).astype(bf16)
    diag = [dot_nn(ref[...], marks) for ref in tables]
    lane = iota((32, 128), 1)

    def shifted(row, rows):
        return pltpu.roll(jnp.broadcast_to(row, (rows, 256)), 0, 1, stride=1, stride_axis=0)[:, 128:256]

    out_ref[...] = jnp.zeros(out_ref.shape, bf16)
    for head in range(HEADS):
        x = jnp.where(lane < 32, shifted(diag[0][head : head + 1, :], 32), 0.0)
        y = jnp.where(lane < 32, shifted(diag[1][head : head + 1, :], 32), 0.0)
        out_ref[head, 0:32, 0:128] = (x + pltpu.roll(x, 64, 1)).astype(bf16)
        out_ref[head, 32:64, 0:128] = (pltpu.roll(y, 32, 1) + pltpu.roll(y, 96, 1)).astype(bf16)
        out_ref[head, 128:256, 128:256] = shifted(diag[2][head : head + 1, :], 128).astype(bf16)


def consts(vectors, b_up, tables):
    width = vectors[0].shape[0]
    return fetching(
        consts_kernel, 2, (), (*vectors, b_up, *tables),
        [((HEADS, 256, 256), bf16), ((8, width), f32), ((1, b_up.shape[0]), f32)],
    )


def pick_kernel(d_ref, wk_ref, wv_ref, wq_ref, vec_ref, wo_ref, warr_ref, barr_ref, oarr_ref):
    head = d_ref[0] * (HEADS // 4) + pl.program_id(0)
    even = (head % 2) == 0
    low = lane_low()

    def arrange(k, v, q):
        k_low = jnp.where(even, k, pltpu.roll(k, 64, 1))
        v_high = jnp.where(even, pltpu.roll(v, 64, 1), v)
        q_low = jnp.where(even, q, pltpu.roll(q, 64, 1))
        return jnp.concatenate([jnp.where(low, k_low, v_high), jnp.where(low, q_low, 0.0)], axis=1)

    warr_ref[...] = arrange(
        wk_ref[...].astype(f32), wv_ref[...].astype(f32), wq_ref[...].astype(f32)
    ).astype(bf16)
    bv = jnp.broadcast_to(vec_ref[7:8, :], (8, 128))
    bq = jnp.broadcast_to(vec_ref[6:7, :], (8, 128))
    barr_ref[...] = arrange(jnp.zeros_like(bv), bv, bq)
    oarr_ref[0:64, :] = jnp.zeros((64, oarr_ref.shape[1]), bf16)
    oarr_ref[64:128, :] = wo_ref[...]


def pick_weights(scalars, w_key, w_value, w_query, vec, w_out):
    width = w_key.shape[0]
    own = HEADS // 4
    pair = lambda i, d: (0, (d[0] * own + i) // 2)
    return pl.pallas_call(
        pick_kernel,
        cost_estimate=cost(2),
        grid_spec=pltpu.PrefetchScalarGridSpec(
            num_scalar_prefetch=1,
            grid=(own,),
            in_specs=[pl.BlockSpec((width, 128), pair)] * 3
            + [pl.BlockSpec((8, 128), pair)]
            + [pl.BlockSpec((64, width), lambda i, d: (d[0] * own + i, 0))],
            out_specs=[
                pl.BlockSpec((width, 256), lambda i, d: (0, i)),
                pl.BlockSpec((8, 256), lambda i, d: (0, i)),
                pl.BlockSpec((128, width), lambda i, d: (i, 0)),
            ],
        ),
        out_shape=[
            struct((width, own * 256), bf16),
            struct((8, own * 256), f32),
            struct((own * 128, width), bf16),
        ],
        compiler_params=params(SCOPED_MB),
    )(scalars, w_key, w_value, w_query, vec, w_out)


def proj_kernel(with_query, first, d_ref, a_ref, b_ref, wk_ref, wv_ref, vec_ref, *refs):
    if with_query:
        wq_ref, k_ref, v_ref, hot_ref, h0_ref, q_ref = refs
    else:
        k_ref, v_ref, hot_ref, h0_ref = refs
    rows = a_ref.shape[0] - BOX_ROWS
    lane = iota((rows, 256), 1)
    for n, ref in enumerate((a_ref, b_ref)):
        h0_ref[n * rows : (n + 1) * rows, :] = ref[0:rows, :]
        boxes = ref[rows : rows + BOX_ROWS, 0:rows].astype(f32).T
        level = jnp.floor(boxes * (1.0 / level_step)).astype(i32)
        start = (d_ref[0] ^ (first + n)) * rows
        place = (start + iota((rows, 256), 0)) // level_step + 128
        flat = jnp.where(lane % 64 < 32, level[:, 0:1], level[:, 1:2] + 32) + (lane // 64) * 64
        want = jnp.where(lane >= 128, place, flat)
        hot_ref[n * rows : (n + 1) * rows, :] = (want == lane).astype(bf16)
    h0 = h0_ref[...]
    width = h0.shape[1]
    for c in range(0, width, 256):
        part = slice(c, c + 256)
        k_ref[:, part] = dot_nn(h0, wk_ref[:, part]).astype(bf16)
        v_ref[:, part] = (dot_nn(h0, wv_ref[:, part]) + vec_ref[7:8, part]).astype(bf16)
        if with_query:
            query = dot_nn(h0[0:rows, :], wq_ref[:, part]) + vec_ref[6:7, part]
            q_ref[:, part] = query.astype(bf16) * bf16(0.125)


def project(scalars, msg_a, msg_b, w_key, w_value, vec, first, w_query=None):
    rows = msg_a.shape[0] - BOX_ROWS
    width = msg_a.shape[1]
    keys = 2 * rows
    args = [scalars, msg_a, msg_b, w_key, w_value, vec]
    outs = [((keys, width), bf16), ((keys, width), bf16), ((keys, 256), bf16), ((keys, width), bf16)]
    if w_query is not None:
        args.append(w_query)
        outs.append(((rows, width), bf16))
    kernel = functools.partial(proj_kernel, w_query is not None, first)
    return resident(kernel, 2, args, outs)


def norm_parts(resid):
    center = resid - jnp.mean(resid, axis=-1, keepdims=True)
    spread = jnp.mean(center * center, axis=-1, keepdims=True)
    rstd = lax.rsqrt(spread + norm_eps)
    return center * rstd, rstd


def place_mask(d_ref, rows, first, shape, dim):
    place = (d_ref[0] ^ first) * rows + iota(shape, dim)
    live = jnp.logical_or(place >= 2 * rows, place < d_ref[1])
    return jnp.where(live, 0.0, masked_score).astype(f32)


def query_classes(e, q_pair, hot_own, bias):
    low = lane_low()
    mine = low if e == 0 else jnp.logical_not(low)
    side = dot_nn(hot_own, bias).astype(bf16)
    return jnp.concatenate([jnp.where(mine, q_pair, side[:, 0:128]), side[:, 128:256]], axis=1)


def pair_scores(e, q_aug, k_pair, hot_ref, mask):
    low = lane_low()
    mine = low if e == 0 else jnp.logical_not(low)
    k_aug = jnp.concatenate([jnp.where(mine, k_pair, hot_ref[:, 0:128]), hot_ref[:, 128:256]], axis=1)
    return dot_nt(q_aug, k_aug) + mask, mine


def attn_near_kernel(d_ref, q_ref, k_ref, v_ref, hot_ref, b_ref, acc_ref, top_ref, aug_ref):
    rows = q_ref.shape[0]
    low = lane_low()
    mask = jnp.concatenate([place_mask(d_ref, rows, b, (1, rows), 1) for b in (0, 1)], axis=1)
    hot_own = hot_ref[0:rows, :]

    for head in range(HEADS):
        pair = slice(128 * (head // 2), 128 * (head // 2 + 1))
        aug_ref[head] = query_classes(head % 2, q_ref[:, pair], hot_own, b_ref[head])

    def scores(head):
        pair = slice(128 * (head // 2), 128 * (head // 2 + 1))
        return pair_scores(head % 2, aug_ref[head], k_ref[:, pair], hot_ref, mask)

    ahead = scores(0)
    tops = []
    for head in range(HEADS):
        pair = slice(128 * (head // 2), 128 * (head // 2 + 1))
        score, mine = ahead
        if head + 1 < HEADS:
            ahead = scores(head + 1)
        top = jnp.max(score, axis=1, keepdims=True)
        weight = jnp.exp(score - top).astype(bf16)
        acc_ref[head] = dot_nn(weight, jnp.where(mine, v_ref[:, pair], bf16(1)))
        tops.append(top)
        if head % 2:
            top_ref[:, pair] = jnp.where(low, tops[-2], tops[-1])


def attn_far_kernel(
    d_ref, aug_ref, k_ref, v_ref, hot_ref, acc_ref, top_ref, h0_ref, wout_ref, vec_ref,
    r1_ref, h1_ref, h1r_ref, ctx_s,
):
    rows = aug_ref.shape[1]
    low = lane_low()
    mask = jnp.concatenate([place_mask(d_ref, rows, b, (1, rows), 1) for b in (2, 3)], axis=1)
    def scores(head):
        pair = slice(128 * (head // 2), 128 * (head // 2 + 1))
        return pair_scores(head % 2, aug_ref[head], k_ref[:, pair], hot_ref, mask)

    ahead = scores(0)
    outs = []
    for head in range(HEADS):
        pair = slice(128 * (head // 2), 128 * (head // 2 + 1))
        score, mine = ahead
        if head + 1 < HEADS:
            ahead = scores(head + 1)
        old_top = top_ref[:, 64 * head : 64 * head + 1]
        top = jnp.maximum(jnp.max(score, axis=1, keepdims=True), old_top)
        weight = jnp.exp(score - top).astype(bf16)
        acc = dot_nn(weight, jnp.where(mine, v_ref[:, pair], bf16(1)))
        acc = acc + acc_ref[head] * jnp.exp(old_top - top)
        outs.append(acc / pltpu.roll(acc, 64, 1))
        if head % 2:
            ctx_s[:, pair] = jnp.where(low, outs[-2], outs[-1]).astype(bf16)
    resid = h0_ref[...] + (dot_nn(ctx_s[...], wout_ref[...]) + vec_ref[0:1, :])
    r1_ref[...] = resid
    hidden = norm_parts(resid)[0] * vec_ref[1:2, :] + vec_ref[2:3, :]
    h1_ref[...] = hidden
    h1r_ref[...] = hidden.astype(bf16)


def attn_near(scalars, q, k, v, hot, bias):
    rows, width = q.shape
    return resident(
        attn_near_kernel, 5, (scalars, q, k, v, hot, bias),
        [((HEADS, rows, 128), f32), ((rows, width), f32), ((HEADS, rows, 256), bf16)],
    )


def attn_far(scalars, aug, k, v, hot, acc, top, h0, w_out, vec):
    rows, width = h0.shape
    return resident(
        attn_far_kernel, 7,
        (scalars, aug, k, v, hot, acc, top, h0, w_out, vec),
        [((rows, width), f32), ((rows, width), f32), ((rows, width), bf16)],
        [((rows, width), bf16)],
    )


def gelu_parts(u):
    phi = 0.5 + 0.5 * lax.erf(u * 0.7071067811865476)
    dens = jnp.exp(-0.5 * (u * u)) * 0.3989422804014327
    return u * phi, phi + u * dens


def norm_back(grad, xhat, rstd, gain):
    scaled = grad * gain
    mean_a = jnp.mean(scaled, axis=-1, keepdims=True)
    mean_b = jnp.mean(scaled * xhat, axis=-1, keepdims=True)
    return rstd * (scaled - mean_a - xhat * mean_b)


def col_sum(values):
    return jnp.sum(values, axis=0, keepdims=True)


def ffn_fwd_kernel(
    h1r_ref, wup_ref, bup_ref, wdown_ref, h1_ref, cot_ref, vec_ref,
    out_ref, dy_ref, dr2_ref, gp_ref, sums_ref,
):
    width = h1_ref.shape[1]
    h1r = h1r_ref[...]
    total = vec_ref[3:4, :]
    hidden = wup_ref.shape[1]
    ahead = dot_nn(h1r, wup_ref[:, 0:width])
    for c in range(0, hidden, width):
        part = slice(c, c + width)
        u = ahead
        if c + width < hidden:
            ahead = dot_nn(h1r, wup_ref[:, c + width : c + 2 * width])
        g, slope = gelu_parts(u + bup_ref[0:1, part])
        gp_ref[:, part] = slope.astype(bf16)
        total = total + dot_nn(g.astype(bf16), wdown_ref[part, :])
    gain = vec_ref[4:5, :]
    xhat, rstd = norm_parts(h1_ref[...] + total)
    out_ref[0, 0] = (xhat * gain + vec_ref[5:6, :]).astype(bf16)
    grad = cot_ref[0, 0].astype(f32)
    dr2 = norm_back(grad, xhat, rstd, gain)
    dr2_ref[...] = dr2
    dy = dr2.astype(bf16)
    dy_ref[...] = dy
    sums_ref[0:1, :] = col_sum(dy.astype(f32))
    sums_ref[1:2, :] = col_sum(grad * xhat)
    sums_ref[2:3, :] = col_sum(grad)
    sums_ref[3:8, :] = jnp.zeros((5, width), f32)


def ffn_fwd(h1r, w_up, b_up, w_down, h1, cot, vec):
    rows, width = h1.shape
    return resident(
        ffn_fwd_kernel, 5, (h1r, w_up, b_up, w_down, h1, cot, vec),
        [
            (cot.shape, bf16), ((rows, width), bf16), ((rows, width), f32),
            ((rows, w_up.shape[1]), bf16), ((8, width), f32),
        ],
        scalars=0,
    )


def ffn_bwd_kernel(
    dy_ref, wdown_ref, gp_ref, wup_ref, dr2_ref, r1_ref, vec_ref, dr1_ref, da_ref, sums_ref
):
    width = dr2_ref.shape[1]
    dy = dy_ref[...]
    grad = dr2_ref[...]
    hidden = wup_ref.shape[1]
    ahead = dot_nt(dy, wdown_ref[0:width, :])
    for c in range(0, hidden, width):
        part = slice(c, c + width)
        dg = ahead
        if c + width < hidden:
            ahead = dot_nt(dy, wdown_ref[c + width : c + 2 * width, :])
        du = (dg * gp_ref[:, part].astype(f32)).astype(bf16)
        grad = grad + dot_nt(du, wup_ref[:, part])
    xhat, rstd = norm_parts(r1_ref[...])
    dr1 = norm_back(grad, xhat, rstd, vec_ref[1:2, :])
    dr1_ref[...] = dr1
    da = dr1.astype(bf16)
    da_ref[...] = da
    sums_ref[0:1, :] = col_sum(da.astype(f32))
    sums_ref[1:2, :] = col_sum(grad * xhat)
    sums_ref[2:3, :] = col_sum(grad)
    sums_ref[3:4, :] = col_sum(dr1)
    sums_ref[4:8, :] = jnp.zeros((4, width), f32)


def ffn_bwd(dy, w_down, gp, w_up, dr2, r1, vec):
    rows, width = dr2.shape
    return resident(
        ffn_bwd_kernel, 1, (dy, w_down, gp, w_up, dr2, r1, vec),
        [((rows, width), f32), ((rows, width), bf16), ((8, width), f32)],
        scalars=0,
    )


def quarters_kernel(d_ref, wup_ref, wdown_ref, up_ref, down_ref):
    size = up_ref.shape[1]
    own = pl.ds(pl.multiple_of(d_ref[0] * size, 128), size)
    up_ref[...] = wup_ref[:, own]
    down_ref[...] = wdown_ref[own, :]


def own_quarters(scalars, w_up, w_down):
    width, hidden = w_up.shape
    size = hidden // 4
    return resident(
        quarters_kernel, 0.5, (scalars, w_up, w_down), [((width, size), bf16), ((size, width), bf16)]
    )


def ffn_again_kernel(d_ref, *refs):
    h1_refs, (wup_ref, bup_ref, g_ref, gp_ref) = refs[:4], refs[4:]
    rows = h1_refs[0].shape[0]
    part = g_ref.shape[1]
    w_up = wup_ref[...]
    b_up = bup_ref[0:1, pl.ds(pl.multiple_of(d_ref[0] * part, 128), part)]
    ahead = dot_nn(h1_refs[0][...], w_up)
    for b in range(4):
        u = ahead
        if b < 3:
            ahead = dot_nn(h1_refs[b + 1][...], w_up)
        g, slope = gelu_parts(u + b_up)
        g_ref[b * rows : (b + 1) * rows, :] = g.astype(bf16)
        gp_ref[b * rows : (b + 1) * rows, :] = slope.astype(bf16)


def ffn_again(scalars, h1_blocks, up_own, b_up):
    rows = h1_blocks[0].shape[0]
    part = up_own.shape[1]
    return resident(
        ffn_again_kernel, 2, (scalars, *h1_blocks, up_own, b_up), [((4 * rows, part), bf16)] * 2
    )


def bit_of(d_ref, bit):
    return (d_ref[3] >> bit) & 1


def store_shares(bit, pieces, send_ref, keep_ref):
    half = len(pieces) // 2
    for mine in (0, 1):

        @pl.when(bit == mine)
        def _():
            for n, piece in enumerate(pieces):
                ref = keep_ref if n // half == mine else send_ref
                ref[n % half] = piece()


def owner_order(pages, bits):
    count = len(bits)
    return [sum(((n >> (count - 1 - k)) & 1) << bit for k, bit in enumerate(bits)) for n in range(pages)]


def down_kernel(bit, order, d_ref, g_ref, *refs):
    ctx_refs, dy_refs, da_refs, (send_ref, keep_ref, dy_s, da_s, res_s) = refs[:3], refs[3:7], refs[7:11], refs[11:]
    rows, width = dy_refs[0].shape
    for b in range(4):
        dy_s[b * rows : (b + 1) * rows, :] = dy_refs[b][...]
        da_s[b * rows : (b + 1) * rows, :] = da_refs[b][...]
    size = g_ref.shape[1]
    for n in range(0, size, 256):
        res_s[n : n + 256, :] = dot_tn(g_ref[:, n : n + 256], dy_s[...]).astype(bf16)
    ctx = jnp.concatenate([ref[...] for ref in ctx_refs], axis=0)
    res_s[size:, :] = dot_nn(ctx, da_s[...]).astype(bf16)
    pages = len(order)
    down, out = size // pages, ctx.shape[0] // pages

    def piece(owner):
        return lambda: jnp.concatenate(
            [
                res_s[owner * down : (owner + 1) * down, :].astype(f32),
                res_s[size + owner * out : size + (owner + 1) * out, :].astype(f32),
            ],
            axis=0,
        ).astype(bf16)

    store_shares(bit_of(d_ref, bit), [piece(owner) for owner in order], send_ref, keep_ref)


def down_grad(scalars, bit, order, g_q, ctxs, dy_blocks, da_blocks):
    rows, width = dy_blocks[0].shape
    size, out = g_q.shape[1], len(ctxs) * ctxs[0].shape[0]
    pages = len(order)
    share = ((pages // 2, (size + out) // pages, width), bf16)
    return resident(
        functools.partial(down_kernel, bit, order), 0.02, (scalars, g_q, *ctxs, *dy_blocks, *da_blocks),
        [share, share],
        [((4 * rows, width), bf16), ((4 * rows, width), bf16), ((size + out, width), bf16)],
    )


def up_kernel(bit, order, d_ref, gp_ref, wdown_ref, *refs):
    dy_refs, h1_refs, (send_ref, keep_ref, sums_ref, du_s, h1_s, res_s) = refs[:4], refs[4:8], refs[8:]
    rows, width = dy_refs[0].shape
    w_down = wdown_ref[...]
    for b in range(4):
        part = slice(b * rows, (b + 1) * rows)
        du = (dot_nt(dy_refs[b][...], w_down) * gp_ref[part, :].astype(f32)).astype(bf16)
        du_s[part, :] = du
        h1_s[part, :] = h1_refs[b][...]
        total = col_sum(du.astype(f32))
        sums = total if b == 0 else sums + total
    sums_ref[...] = jnp.broadcast_to(sums, sums_ref.shape)
    for n in range(0, width, 256):
        res_s[n : n + 256, :] = dot_tn(h1_s[:, n : n + 256], du_s[...])
    pages = len(order)
    own = width // 4
    rows = own // pages

    def piece(owner):
        starts = [q * own + owner * rows for q in (0, 2, 1, 3)]
        return lambda: jnp.stack([res_s[n : n + rows, :].astype(bf16) for n in starts])

    store_shares(bit_of(d_ref, bit), [piece(owner) for owner in order], send_ref, keep_ref)


def up_grad(scalars, bit, order, gp_q, down_own, dy_blocks, h1_blocks):
    rows, width = dy_blocks[0].shape
    part = gp_q.shape[1]
    pages = len(order)
    share = ((pages // 2, 4, width // 4 // pages, part), bf16)
    return resident(
        functools.partial(up_kernel, bit, order), 2,
        (scalars, gp_q, down_own, *dy_blocks, *h1_blocks),
        [share, share, ((8, part), f32)],
        [((4 * rows, part), bf16), ((4 * rows, width), bf16), ((width, part), f32)],
    )


def step_kernel(bit, d_ref, keep_ref, got_ref, *out_refs):
    half = keep_ref.shape[0] // 2
    mine = bit_of(d_ref, bit)
    for ref, at in zip(out_refs, (1 - mine, mine)):
        part = pl.ds(at * half, half)
        ref[...] = (keep_ref[part].astype(f32) + got_ref[part].astype(f32)).astype(bf16)


def step_sum(scalars, bit, keep, got):
    half = (keep.shape[0] // 2,) + keep.shape[1:]
    kernel = functools.partial(step_kernel, bit)
    return resident(kernel, 0.02, (scalars, keep, got), [(half, bf16)] * 2)


def last_kernel(keep_ref, got_ref, out_ref):
    out_ref[...] = (keep_ref[0].astype(f32) + got_ref[0].astype(f32)).astype(bf16)


def last_sum(keep, got):
    return resident(last_kernel, 0.02, (keep, got), [(keep.shape[1:], bf16)], scalars=0)[0]


def cross_kernel(bit, d_ref, keep_ref, got_ref, *out_refs):
    page, stream = bit_of(d_ref, bit), d_ref[4]
    places = ((page, stream), (1 - page, stream), (page, 1 - stream), (1 - page, 1 - stream))
    for ref, (at, way) in zip(out_refs, places):
        for seq in (0, 1):
            total = keep_ref[at, 2 * seq + way].astype(f32) + got_ref[at, 2 * seq + way].astype(f32)
            ref[seq] = total.astype(bf16)


def cross(scalars, bit, keep, got):
    shape = (2,) + keep.shape[2:]
    kernel = functools.partial(cross_kernel, bit)
    return resident(kernel, 0.02, (scalars, keep, got), [(shape, bf16)] * 4)


def turn_kernel(d_ref, keep_ref, page_ref, stream_ref, both_ref, send_ref, stay_ref):
    for ref, seq in ((send_ref, 1 - d_ref[5]), (stay_ref, d_ref[5])):
        ref[0] = (keep_ref[seq].astype(f32) + page_ref[seq].astype(f32)).astype(bf16)
        ref[1] = (stream_ref[seq].astype(f32) + both_ref[seq].astype(f32)).astype(bf16)


def turn(scalars, pieces):
    return resident(turn_kernel, 0.02, (scalars, *pieces), [(pieces[0].shape, bf16)] * 2)


def quarters_join_kernel(own_ref, near_ref, out_ref):
    for k in (0, 1):
        out_ref[0, 2 * k] = own_ref[k]
        out_ref[0, 2 * k + 1] = near_ref[k]


def quarters_join(own, near):
    shape = (1, 4) + own.shape[1:]
    return resident(quarters_join_kernel, 0.02, (own, near), [(shape, bf16)], scalars=0)[0]


def join_kernel(one_ref, two_ref, out_ref):
    half = one_ref.shape[0]
    out_ref[0:half] = one_ref[...]
    out_ref[half:] = two_ref[...]


def join(one, two):
    shape = (2 * one.shape[0],) + one.shape[1:]
    return resident(join_kernel, 0.02, (one, two), [(shape, bf16)], scalars=0)[0]


def weights_kernel(
    head, d_ref, h0a_ref, h0b_ref, warr_ref, barr_ref, hota_ref, hotb_ref, b_ref,
    p_ref, kat_ref, et_ref, r_ref, ctx_ref, e_s,
):
    rows = h0a_ref.shape[0] // 2
    half = 2 * rows
    low = lane_low()
    one = jnp.ones((), bf16)
    mask = jnp.concatenate([place_mask(d_ref, rows, b, (1, rows), 1) for b in range(4)], axis=1)
    hots = (hota_ref, hotb_ref)
    cols = slice(256 * head, 256 * (head + 1))
    for n, ref in enumerate((h0a_ref, h0b_ref)):
        part = slice(half * n, half * (n + 1))
        p_ref[part, :] = (dot_nn(ref[...], warr_ref[:, cols]) + barr_ref[0:1, cols]).astype(bf16)
    kv = p_ref[:, 0:128]
    hot = jnp.concatenate([hota_ref[...], hotb_ref[...]], axis=0)
    k_aug = jnp.concatenate([jnp.where(low, kv, hot[:, 0:128]), hot[:, 128:256]], axis=1)
    kat_ref[...] = k_aug.T
    v_one_t = jnp.where(low, one, kv).T
    bias = b_ref[d_ref[0] * (HEADS // 4) + head]
    side = dot_nn(hot, bias).astype(bf16)
    q_only = p_ref[:, 128:256] * bf16(0.125)
    q_aug = jnp.concatenate([jnp.where(low, q_only, side[:, 0:128]), side[:, 128:256]], axis=1)
    ahead = dot_nt(q_aug[0:rows], k_aug) + mask
    for block in range(4):
        part = slice(rows * block, rows * (block + 1))
        score = ahead
        if block < 3:
            ahead = dot_nt(q_aug[rows * (block + 1) : rows * (block + 2)], k_aug) + mask
        top = jnp.max(score, axis=1, keepdims=True)
        weight = jnp.exp(score - top).astype(bf16)
        e_s[part, :] = weight
    et_ref[...] = e_s[...].T
    acc = dot_nt(v_one_t, e_s[...])
    recip = 1.0 / acc[0:8, :]
    r_ref[...] = recip
    ctx_ref[...] = (acc[64:128, :] * recip[0:1, :]).astype(bf16)


def own_weights(head, scalars, h0_near, h0_far, w_arr, b_arr, hot_near, hot_far, bias):
    keys = 2 * h0_near.shape[0]
    return resident(
        functools.partial(weights_kernel, head), 1,
        (scalars, h0_near, h0_far, w_arr, b_arr, hot_near, hot_far, bias),
        [
            ((keys, 256), bf16), ((256, keys), bf16), ((keys, keys), bf16), ((8, keys), f32),
            ((64, keys), bf16),
        ],
        [((keys, keys), bf16)],
    )


def turned_kernel(near_ref, far_ref, out_ref):
    half = near_ref.shape[0]
    out_ref[:, 0:half] = near_ref[...].T
    out_ref[:, half:] = far_ref[...].T


def transposed(near, far):
    return resident(
        turned_kernel, 0.5, (near, far), [((near.shape[1], 2 * near.shape[0]), bf16)], scalars=0
    )[0]


def attn_bwd_kernel(head, h0t_ref, *refs):
    da_refs = refs[:4]
    p_ref, kat_ref, et_ref, r_ref, warr_ref, oarr_ref, hota_ref, hotb_ref = refs[4:12]
    dp_ref, dw_ref, tab_ref, row_ref, ds_s, dc_s = refs[12:]
    rows, width = da_refs[0].shape
    keys = 4 * rows
    low = lane_low()
    zero = jnp.zeros((), bf16)
    cols = slice(256 * head, 256 * (head + 1))
    v_only = jnp.where(low, zero, p_ref[:, 0:128])
    k_aug_t = kat_ref[...]
    oarr = oarr_ref[128 * head : 128 * (head + 1), :]
    w_arr = warr_ref[:, cols]
    for block in range(4):
        part = slice(rows * block, rows * (block + 1))
        dc = dot_nt(da_refs[block][...], oarr) * r_ref[:, part].T[:, 0:1]
        dc_s[part, :] = dc.astype(bf16)
    ahead = dot_nt(v_only, dc_s[0:rows, :])
    for block in range(4):
        part = slice(rows * block, rows * (block + 1))
        recip = r_ref[:, part]
        weight = et_ref[:, part].astype(f32)
        dweight = ahead
        if block < 3:
            ahead = dot_nt(v_only, dc_s[rows * (block + 1) : rows * (block + 2), :])
        inner = jnp.sum(weight * dweight, axis=0, keepdims=True) * recip[0:1, :]
        ds_s[:, part] = (weight * (dweight - inner)).astype(bf16)
    q_only = p_ref[:, 128:256] * bf16(0.125)
    dp_ref[:, 0:128] = (dot_nn(ds_s[...], q_only) + dot_nn(et_ref[...], dc_s[...])).astype(bf16)
    dq_aug_t = dot_nn(k_aug_t, ds_s[...])
    dq = dq_aug_t[0:128, :].T * 0.125
    dp_ref[:, 128:256] = jnp.where(low, dq, 0.0).astype(bf16)
    dq_aug_t = dq_aug_t.astype(bf16)
    half = 2 * rows
    acc_b = dot_nn(dq_aug_t[:, :half], hota_ref[...]) + dot_nn(dq_aug_t[:, half:], hotb_ref[...])
    dp = dp_ref[...]
    dw_ref[...] = dot_nn(h0t_ref[...], dp)
    total = col_sum(dp.astype(f32))
    row_ref[...] = jnp.zeros(row_ref.shape, f32)
    row_ref[0:1, 0:256] = total
    high = total.astype(bf16)
    rest = (total - high.astype(f32)).astype(bf16)
    lang = dot_nt(jnp.broadcast_to(high, (8, 256)), w_arr)
    lang = lang + dot_nt(jnp.broadcast_to(rest, (8, 256)), w_arr)
    row_ref[1:2, :] = lang[0:1, :]
    for first, block in (
        (0, acc_b[64:96, 0:128]), (32, acc_b[96:128, 0:128]), (64, acc_b[128:256, 128:256]),
    ):
        size = block.shape[0]
        lane = iota((size, 128), 1)
        key = iota((size, 128), 0)
        if first == 32:
            lane = lane - 32
        index = jnp.clip(key - lane, -16, 15) + 16
        if size == 32:
            index = jnp.where(jnp.logical_and(lane >= 0, lane < 32), index, -1)
        for bucket in range(32):
            at = first + bucket
            tab_ref[at : at + 1, :] = col_sum(jnp.where(index == bucket, block, 0.0))


def attn_bwd(head, h0_t, da_blocks, p_all, kat, et, recip, w_arr, o_arr, hot_near, hot_far):
    rows, width = da_blocks[0].shape
    keys = 4 * rows
    return resident(
        functools.partial(attn_bwd_kernel, head), 0.02,
        (h0_t, *da_blocks, p_all, kat, et, recip, w_arr, o_arr, hot_near, hot_far),
        [((keys, 256), bf16), ((width, 256), f32), ((96, 128), f32), ((8, width), f32)],
        [((keys, keys), bf16), ((keys, 128), bf16)], scalars=0,
    )


def input_kernel(*refs):
    dp_refs, (warr_ref, dr1_ref, own_ref, near_ref, far_ref) = refs[:3], refs[3:]
    rows = dr1_ref.shape[0]
    dp = jnp.concatenate([ref[...] for ref in dp_refs], axis=1)
    for b in (1, 3, 2, 0):
        part = dot_nt(dp[b * rows : (b + 1) * rows, :], warr_ref[...])
        if b == 0:
            own_ref[...] = dr1_ref[...] + part
        elif b == 2:
            far_ref[...] = part
        else:
            near_ref[(b // 2) * rows : (b // 2 + 1) * rows, :] = part.astype(bf16)


def input_parts(dps, w_arr, dr1):
    rows, width = dr1.shape
    return resident(
        input_kernel, 0.02, (*dps, w_arr, dr1),
        [((rows, width), f32), ((2 * rows, width), bf16), ((rows, width), f32)], scalars=0,
    )


def far_kernel(part_ref, got_ref, out_ref):
    rows = part_ref.shape[0]
    out_ref[...] = (part_ref[...] + got_ref[rows:, :].astype(f32)).astype(bf16)


def far_share(far_part, got_near):
    return resident(far_kernel, 0.02, (far_part, got_near), [(far_part.shape, bf16)], scalars=0)[0]


def input_sum_kernel(own_ref, near_ref, far_ref, out_ref):
    rows = own_ref.shape[0]
    total = own_ref[...] + near_ref[0:rows, :].astype(f32) + far_ref[...].astype(f32)
    out_ref[0, 0] = total.astype(bf16)


def input_sum(own_part, got_near, got_far):
    shape = (1, 1) + own_part.shape
    return resident(
        input_sum_kernel, 0.02, (own_part, got_near, got_far), [(shape, bf16)], scalars=0
    )[0]


SMALL_ROWS = 96


def pack_kernel(bit, order, d_ref, *refs):
    one_ref, two_ref, up_ref = refs[:3]
    dw_refs, row_refs, tab_refs, (send_ref, keep_ref, m_s) = refs[3:6], refs[6:9], refs[9:12], refs[12:]
    quarter, language = d_ref[0], d_ref[2]
    pages = len(order)
    own = HEADS // 4
    cols = own * 64
    n = cols // pages
    m_s[...] = jnp.zeros(m_s.shape, f32)
    lang = one_ref[3:4, :]
    for ref in row_refs:
        lang = lang + ref[1:2, :]
    vectors = [one_ref[k : k + 1, :] for k in range(3)] + [two_ref[k : k + 1, :] for k in range(3)]
    vectors += [None, None, None, None, None, None]
    vectors += [jnp.where(language == k, lang, 0.0) for k in range(7)]
    lane = iota((32, 128), 1)
    tables = [jnp.zeros((32, 128), f32) for _ in range(3)]
    for j in range(own):
        sums = jnp.sum(tab_refs[j][...], axis=1, keepdims=True)
        for t in range(3):
            at = 12 * t + quarter * own + j
            tables[t] = jnp.where(lane == at, sums[32 * t : 32 * (t + 1), :], tables[t])
    table = tables[0] + tables[1] + tables[2]
    for q in range(4):
        mine = quarter == q
        for k, vector in enumerate(vectors):
            if vector is not None:
                for part in range(own):
                    first = q * cols + 64 * part
                    m_s[q, 3 * k + part : 3 * k + part + 1, 0:64] = vector[:, first : first + 64]
        for j in range(own):
            row = row_refs[j]
            m_s[q, 18 + j : 19 + j, 0:64] = jnp.where(mine, row[0:1, 128:192], 0.0)
            m_s[q, 21 + j : 22 + j, 0:64] = jnp.where(mine, row[0:1, 64:128], 0.0)
        for k in range(12):
            m_s[q, 24 + k : 25 + k, 0:64] = jnp.where(mine, up_ref[0:1, 64 * k : 64 * (k + 1)], 0.0)
        m_s[q, 64:72, 0:64] = table[8 * q : 8 * (q + 1), 0:64]
    share = SMALL_ROWS // pages
    zeros = jnp.zeros((n - share, 64), f32)

    def block(p, q):
        first = q * cols + p * n
        pieces = [ref[first : first + n, 64 * t : 64 * (t + 1)] for t in range(3) for ref in dw_refs]
        small = m_s[q, p * share : (p + 1) * share, 0:64]
        pieces.append(jnp.concatenate([small, zeros], axis=0))
        return jnp.concatenate(pieces, axis=1).astype(bf16)

    def piece(p):
        return lambda: jnp.stack([block(p, q) for q in (0, 2, 1, 3)])

    store_shares(bit_of(d_ref, bit), [piece(p) for p in order], send_ref, keep_ref)


def pack(scalars, bit, order, sums_one, sums_two, sums_up, dws, rows_out, tabs):
    pages = len(order)
    n = dws[0].shape[0] // 4 // pages
    return resident(
        functools.partial(pack_kernel, bit, order), 0.02,
        (scalars, sums_one, sums_two, sums_up, *dws, *rows_out, *tabs),
        [((pages // 2, 4, n, 640), bf16)] * 2, [((4, SMALL_ROWS, 128), f32)],
    )


def heads_kernel(distances, d_ref, *refs):
    got_refs, (key_ref, value_ref, query_ref, small_s) = parts_of(refs[:-4]), refs[-4:]
    pages = len(got_refs)
    share = SMALL_ROWS // pages
    for ref, distance in zip(got_refs, distances):
        page = d_ref[3] ^ distance
        blocks = [ref[d_ref[0] ^ q].astype(f32) for q in range(4)]
        for t, out_ref in enumerate((key_ref, value_ref, query_ref)):
            out_ref[page] = jnp.concatenate(
                [block[:, 192 * t : 192 * (t + 1)] for block in blocks], axis=1
            )
        total = (blocks[0] + blocks[1]) + (blocks[2] + blocks[3])
        small_s[page, :, 0:64] = total[0:share, 576:640]


def small_kernel(m_ref, *refs):
    vec_refs, (up_ref, lang_ref, x_ref, y_ref, pos_ref, m_s) = refs[:8], refs[8:]
    pages, share, _ = m_ref.shape
    for p in range(pages):
        m_s[p * share : (p + 1) * share, :] = m_ref[p]

    def row(first, count):
        parts = [m_s[first + k : first + k + 1, 0:64] for k in range(count)]
        return jnp.concatenate(parts, axis=1).reshape(64 * count)

    for k, ref in enumerate(vec_refs):
        ref[...] = row(3 * k, 3)
    up_ref[...] = row(24, 12)
    for part in range(3):
        piece = jnp.concatenate(
            [m_s[36 + 3 * k + part : 37 + 3 * k + part, 0:64] for k in range(7)] + [jnp.zeros((1, 64), f32)], axis=0
        )
        lang_ref[64 * part : 64 * (part + 1), :] = piece.T[:, 0:7]
    for t, ref in enumerate((x_ref, y_ref, pos_ref)):
        ref[...] = m_s[64:72, 12 * t : 12 * (t + 1)]


def finish_heads(scalars, pieces, distances):
    _, _, n, _ = pieces[0].shape
    pages = len(distances)
    rows = pages * n
    mat = ((pages, n, 4 * rows), f32)
    *mats, small = resident(
        functools.partial(heads_kernel, distances), 0.2, (scalars, *pieces),
        [mat, mat, mat, ((pages, SMALL_ROWS // pages, 128), f32)],
    )
    vecs = resident(
        small_kernel, 0.2, (small,),
        [((rows,), f32)] * 8
        + [((4 * rows,), f32), ((rows, 7), f32)]
        + [((8, HEADS), f32)] * 3,
        [((SMALL_ROWS, 128), f32)], scalars=0,
    )
    return [m.reshape(rows, 4 * rows) for m in mats] + list(vecs)


def parts_of(refs):
    return [ref.at[k] for ref in refs for k in range(ref.shape[0])]


def up_finish_kernel(distances, d_ref, *refs):
    out_ref = refs[-1]
    part = refs[0].shape[-1]
    for ref, distance in zip(parts_of(refs[:-1]), distances):
        for q in range(4):
            cols = pl.ds(pl.multiple_of((d_ref[0] ^ q) * part, 128), part)
            out_ref[d_ref[3] ^ distance, :, cols] = ref[q].astype(f32)


def finish_up(scalars, pieces, distances):
    _, _, n, part = pieces[0].shape
    pages = len(distances)
    kernel = functools.partial(up_finish_kernel, distances)
    rows = resident(kernel, 0.2, (scalars, *pieces), [((pages, n, 4 * part), f32)])[0]
    return rows.reshape(pages * n, 4 * part)


def down_finish_kernel(distances, d_ref, *refs):
    down_ref, out_ref = refs[-2:]
    down = down_ref.shape[1]
    for ref, distance in zip(parts_of(refs[:-2]), distances):
        owner = d_ref[3] ^ distance
        block = ref[...].astype(f32)
        down_ref[owner] = block[0:down, :]
        out_ref[owner] = block[down:, :]


def finish_down(scalars, pieces, size, out, distances):
    width = pieces[0].shape[2]
    pages = len(distances)
    blocks = resident(
        functools.partial(down_finish_kernel, distances), 0.2, (scalars, *pieces),
        [((pages, size // pages, width), f32), ((pages, out // pages, width), f32)],
    )
    return blocks[0].reshape(size, width), blocks[1].reshape(out, width)


def swap(values, axis, bit=0):
    size = lax.axis_size(axis)
    return lax.ppermute(values, axis, [(i, i ^ (1 << bit)) for i in range(size)])


def page_gather(own):
    near = swap(own, "seq")
    far = swap(own, "stream")
    return [own, near, far, swap(far, "seq")]


OUT_BITS = {'up': (0, 1, 2), 'down': (1, 0, 2), 'head': (0, 1, 2)}
BACK_BITS = {'up': (2, 0, 1), 'down': (2, 1, 0), 'head': (0, 2, 1)}
PLAN = (
    "down", "bwd", "bwd", "up a", "bwd", "pack", "down a", "in", "up c", "head a", "up t", "up j", "down b",
    "head c", "up w", "down l", "head t", "head j", "up x", "down w", "head w", "far", "down x", "head x",
    "sum", "up f", "down f", "head f",
)


def both_swap(values, mask):
    pages = lax.axis_size("page")
    pairs = [(2 * p + k, 2 * (p ^ mask) + 1 - k) for p in range(pages) for k in (0, 1)]
    return lax.ppermute(values, ("page", "stream"), pairs)


def page_xor(values, mask):
    pages = lax.axis_size("page")
    return lax.ppermute(values, "page", [(p, p ^ mask) for p in range(pages)])


def on_device(
    tokens, boxes, text_lengths, language, lang_table, w_query, b_query, w_key, w_value, b_value,
    w_out, b_out, norm1_gain, norm1_bias, w_up, b_up, w_down, b_down, norm2_gain, norm2_bias,
    table_pos, table_x, table_y, cotangent,
):
    rows = tokens.shape[2]
    width = tokens.shape[3]
    head_dim = width // HEADS
    own_heads = HEADS // 4
    own_cols = own_heads * head_dim
    pages = lax.axis_size("page")
    scalars, h0, message = prep(language, text_lengths, tokens, boxes.reshape(2, 1, 1, rows), lang_table.T)
    near_msg, far_msg = swap(message, "seq"), swap(message, "stream")
    bias, vec, b_up_row = consts(
        (b_out, norm1_gain, norm1_bias, b_down, norm2_gain, norm2_bias, b_query, b_value), b_up,
        (table_x.T, table_y.T, table_pos.T),
    )

    k_near, v_near, hot_near, h0_near, q_own = project(
        scalars, message, near_msg, w_key, w_value, vec, 0, w_query
    )
    acc, top, aug = attn_near(scalars, q_own, k_near, v_near, hot_near, bias)
    far_msg = after(far_msg, acc)
    last_msg = swap(far_msg, "seq")
    w_arr, b_arr, o_arr = pick_weights(after(scalars, acc), w_key, w_value, w_query, vec, w_out)
    last_msg = after(last_msg, w_arr)
    k_far, v_far, hot_far, h0_far = project(scalars, far_msg, last_msg, w_key, w_value, vec, 2)
    r1, h1, h1r = attn_far(
        scalars, aug, k_far, v_far, hot_far, acc, top, h0, w_out, vec
    )
    h1_near, h1_far = swap(h1r, "seq"), swap(h1r, "stream")
    layer_out, dy, dr2, gp, sums_two = ffn_fwd(h1r, w_up, b_up_row, w_down, h1, cotangent, vec)
    dy_near, dy_far = swap(dy, "seq"), swap(dy, "stream")
    dr1, da, sums_one = ffn_bwd(dy, w_down, gp, w_up, dr2, r1, vec)
    da_near, da_far = swap(da, "seq"), swap(da, "stream")
    up_own, down_own = own_quarters(after(scalars, da), w_up, w_down)

    def weights(j, order_on):
        return own_weights(
            j, after(scalars, order_on), h0_near, h0_far, w_arr, b_arr, hot_near, hot_far, bias
        )

    own = [weights(0, (da, h1_far))]
    h1_far = after(h1_far, own[0][0])
    h1_blocks = [h1r, h1_near, h1_far, swap(h1_far, "seq")]
    g_q, gp_q = ffn_again(after(scalars, own[0][0]), h1_blocks, up_own, b_up_row)
    own.append(weights(1, g_q))
    own.append(weights(2, own[1][0]))
    dy_far, da_far = after((dy_far, da_far), own[2][0])
    dy_blocks = [dy, dy_near, dy_far, swap(dy_far, "seq")]
    da_blocks = [da, da_near, da_far, swap(da_far, "seq")]
    gp_q = after(gp_q, da_far)

    many = list(range(3, pages.bit_length() - 1))
    out_bits = {name: [*OUT_BITS[name], *many] for name in OUT_BITS}
    back_bits = {name: [*BACK_BITS[name], *many] for name in BACK_BITS}
    orders = {name: owner_order(pages, out_bits[name]) for name in out_bits}
    up_send, up_keep, sums_up = up_grad(
        scalars, out_bits["up"][0], orders["up"], gp_q, down_own, dy_blocks, h1_blocks
    )
    h0_t = transposed(after(h0_near, up_keep), h0_far)
    state, heads, out = {}, [], {}

    def put(name, send, keep):
        state[name] = (keep, page_xor(send, 1 << out_bits[name][0]), 1)
        return keep

    put("up", up_send, up_keep)

    def backward(last):
        p_own, kat, et, recip, _ = own[len(heads)]
        heads.append(
            attn_bwd(
                len(heads), h0_t, da_blocks, p_own, after(kat, last), et, recip, w_arr, o_arr, hot_near, hot_far
            )
        )
        return heads[-1][0]

    def down(last):
        ctxs = [o[4] for o in own]
        return put("down", *down_grad(
            scalars, out_bits["down"][0], orders["down"], after(g_q, last), ctxs, dy_blocks, da_blocks
        ))

    def pack_heads(last):
        _, dws, tabs, rows_out = zip(*heads)
        return put("head", *pack(
            after(scalars, last), out_bits["head"][0], orders["head"], sums_one, sums_two, sums_up, dws, rows_out, tabs
        ))

    def advance(name, last):
        keep, got, at = state[name]
        bit = out_bits[name][at]
        send, keep = step_sum(scalars, bit, *after((keep, got), last))
        state[name] = (keep, page_xor(send, 1 << bit), at + 1)
        return keep

    def begin(name, mine):
        bit = back_bits[name][0]
        state[name] = (mine, page_xor(mine, 1 << bit), 1, [0, 1 << bit])
        return mine

    def widen(name, last):
        mine, got, at, masks = state[name]
        mine = join(*after((mine, got), last))
        bit = back_bits[name][at]
        masks = masks + [mask | 1 << bit for mask in masks]
        state[name] = (mine, page_xor(mine, 1 << bit), at + 1, masks)
        return mine

    def crossed(name, last):
        keep, got, at = state[name]
        bit = out_bits[name][at]
        keep, page_part, stream_part, both = cross(scalars, bit, *after((keep, got), last))
        state[name] = [
            keep, page_xor(page_part, 1 << bit), swap(stream_part, "stream"), both_swap(both, 1 << bit)
        ]
        return keep

    def turned(name, last):
        send, keep = turn(scalars, after(state[name], last))
        state[name] = (keep, swap(send, "seq"))
        return keep

    def turned_back(name, last):
        return begin(name, quarters_join(*after(state[name], last)))

    def added_back(name, last):
        keep, got, _ = state[name]
        return begin(name, last_sum(*after((keep, got), last))[None])

    def inputs(last):
        dps = [head[0] for head in heads]
        out["own"], near_part, out["far"] = input_parts(dps, after(w_arr, last), dr1)
        out["near"] = swap(near_part, "seq")
        return out["own"]

    def inputs_far(last):
        share = far_share(out["far"], after(out["near"], last))
        out["got"] = swap(share, "stream")
        return share

    def inputs_sum(last):
        out["grad"] = input_sum(after(out["own"], last), out["near"], out["got"])
        return out["grad"]

    def finish(name, last):
        mine, got, _, masks = state[name]
        info, got = after((scalars, got), last)
        if name == "up":
            out[name] = finish_up(info, [mine, got], masks)
            return out[name]
        if name == "down":
            out[name] = finish_down(info, [mine, got], w_up.shape[1] // 4, own_cols, masks)
            return out[name][0]
        out[name] = finish_heads(info, [mine, got], masks)
        return out[name][0]

    def more(step):
        def run(name, last):
            last = step(name, last)
            for _ in many:
                last = step(name, last)
            return last

        return run

    steps = {
        "bwd": backward, "down": down, "pack": pack_heads, "in": inputs, "far": inputs_far, "sum": inputs_sum,
    }
    chain_steps = {
        "a": more(advance), "b": advance, "c": crossed, "t": turned, "j": turned_back, "l": added_back,
        "w": widen, "x": more(widen), "f": finish,
    }
    last = h0_t
    for word in PLAN:
        if word in steps:
            last = steps[word](last)
        else:
            name, step = word.split()
            last = chain_steps[step](name, last)
    input_grad, res_up = out["grad"], out["up"]
    res_down, res_out = out["down"]
    res_key, res_value, res_query, *vecs, s_bup, s_lang, s_x, s_y, s_pos = out["head"]
    s_bout, s_g1, s_s1, s_bdown, s_g2, s_s2, s_bq, s_bv = vecs
    return (
        layer_out, input_grad, s_lang, res_query, s_bq, res_key, res_value, s_bv,
        res_out, s_bout, s_g1, s_s1, res_up, s_bup, res_down, s_bdown, s_g2, s_s2, s_pos, s_x, s_y,
    )


def solution(mesh):
    token_spec = P("page", "stream", "seq", None)
    rep = P()
    in_specs = (
        (token_spec, P(None, "page", "stream", "seq"), P("page"), P("page"))
        + (rep,) * 19
        + (token_spec,)
    )
    mat, vec = P(("stream", "seq"), None), P(("stream", "seq"))
    out_specs = (
        token_spec, token_spec, mat, mat, vec, mat, mat, vec, mat, vec, vec, vec,
        mat, vec, mat, vec, vec, vec, mat, mat, mat,
    )
    return jax.shard_map(
        on_device, mesh=mesh, in_specs=in_specs, out_specs=out_specs, check_vma=False
    )
```
